512 devices in a mesh: loop: 4 (over x_hi, core), sub: 16 (over z), tp: 8 (over x_lo, y).
Axes of the slice: x: 4 (x_hi: 2, x_lo: 2; x = x_hi * 2 + x_lo), y: 4, z: 16, core: 2. Of those that a mesh axis runs over, the one named last changes fastest.
Arguments:
- img_feat: bfloat16 [8192, 1152], P(('loop', 'sub'), 'tp'), may hold values from -6 to 6
- txt_feat: bfloat16 [8192, 1152], P(('loop', 'sub'), 'tp'), may hold values from -6 to 6
- img_weight: bfloat16 [1152, 1152], P('tp'), may hold values from -0.1875 to 0.1875
- txt_weight: bfloat16 [1152, 1152], P('tp'), may hold values from -0.1875 to 0.1875
- logit_scale: float32 [1], replicated, may hold values from 50.91169 to 135.7645
- logit_bias: float32 [1], replicated, may hold values from -10 to -6
Outputs:
- img_weight_grad: float32 [1152, 1152], P('tp')
- txt_weight_grad: float32 [1152, 1152], P('tp')
The draws below stay inside these ranges and needn't reach their ends.
All inputs are finite; a program needn't handle non-finite values.
Results may differ from the reference program's by a relative error of at most 0.004.
Values may be sent and summed in bfloat16 or wider, within the bound.
A program may use at most 64 MiB of HBM per device.

```python
import math
import jax
import jax.numpy as jnp
from jax import lax

D = 1152
E = 1152
PAIRS = 8192


def block_levels(stream_key, shape, pieces, low, high):
    factor_of, own = 1.0, jax.random.fold_in(stream_key, 6)
    for position, shards_of in pieces:
        heights = jnp.exp(jax.random.uniform(jax.random.fold_in(own, position), (shards_of,), jnp.float32, low / len(pieces), high / len(pieces)))
        factor_of = factor_of * jnp.repeat(heights, shape[position] // shards_of).reshape([-1 if axis == position else 1 for axis in range(len(shape))])
    return factor_of


def normal_values(stream_key, shape, scale, bound, pieces=(), kind=jnp.bfloat16):
    values = scale * jax.random.normal(stream_key, shape, jnp.float32)
    if pieces:
        values = values * block_levels(stream_key, shape, pieces, -0.22, 0.18)
    return jnp.clip(values, -bound, bound).astype(kind)


def setup_inputs(seed: int = 0) -> dict:
    seeds = jax.random.split(jax.random.key(seed), 7)
    img_feat = normal_values(seeds[0], (PAIRS, D), 1.0, 6.0, ((0, 64), (1, 8)))
    txt_feat = normal_values(seeds[1], (PAIRS, D), 1.0, 6.0, ((0, 64), (1, 8)))
    img_weight = normal_values(seeds[2], (D, E), D ** -0.5, 0.1875, ((0, 8),))
    txt_weight = normal_values(seeds[3], (D, E), D ** -0.5, 0.1875, ((0, 8),))
    logit_scale = jnp.clip(jnp.exp(jax.random.uniform(seeds[4], (1,), jnp.float32, math.log(50.91169), math.log(135.7645))), 50.91169, 135.7645)
    logit_bias = jnp.clip(jax.random.uniform(seeds[5], (1,), jnp.float32, -10.0, -6.0), -10.0, -6.0)
    return {"img_feat": img_feat, "txt_feat": txt_feat, "img_weight": img_weight, "txt_weight": txt_weight, "logit_scale": logit_scale, "logit_bias": logit_bias}


def unit_rows(proj):
    inverse = lax.rsqrt(lax.optimization_barrier(jnp.sum(proj * proj, axis=-1, keepdims=True)) + 1e-06)
    return (proj * inverse, inverse)

def unit_back(unit, inverse, upstream):
    return (upstream - unit * lax.optimization_barrier(jnp.sum(unit * upstream, axis=-1, keepdims=True))) * inverse

def reference(img_feat, txt_feat, img_weight, txt_weight, logit_scale, logit_bias):
    pairs = img_feat.shape[0]
    img_unit, img_inv = unit_rows(jnp.dot(img_feat, img_weight, preferred_element_type=jnp.float32))
    txt_unit, txt_inv = unit_rows(jnp.dot(txt_feat, txt_weight, preferred_element_type=jnp.float32))
    img_emb = img_unit.astype(jnp.bfloat16)
    txt_emb = txt_unit.astype(jnp.bfloat16)
    scale = logit_scale[0]
    bias = logit_bias[0]
    block = math.gcd(pairs, 512)
    count = pairs // block
    text_ids = jnp.arange(pairs, dtype=jnp.int32)

    def step(d_text, inputs):
        emb, start = inputs
        logits = scale * lax.dot_general(emb, txt_emb, (((1,), (1,)), ((), ())), preferred_element_type=jnp.float32) + bias
        ids = start + jnp.arange(block, dtype=jnp.int32)
        positive = ids[:, None] == text_ids[None, :]
        slope = (scale * (jax.nn.sigmoid(logits) - positive.astype(jnp.float32)) / pairs).astype(jnp.bfloat16)
        d_text = d_text + lax.dot_general(slope, emb, (((0,), (0,)), ((), ())), preferred_element_type=jnp.float32)
        d_image = jnp.dot(slope, txt_emb, preferred_element_type=jnp.float32)
        return (d_text, d_image)
    starts = jnp.arange(count, dtype=jnp.int32) * block
    init = jnp.zeros((pairs, img_emb.shape[1]), jnp.float32)
    d_text, d_image = lax.scan(step, init, (img_emb.reshape(count, block, -1), starts))
    d_image = d_image.reshape(pairs, -1)
    img_back = unit_back(img_unit, img_inv, d_image).astype(jnp.bfloat16)
    txt_back = unit_back(txt_unit, txt_inv, d_text).astype(jnp.bfloat16)
    dims = (((0,), (0,)), ((), ()))
    img_grad = lax.dot_general(img_feat, img_back, dims, preferred_element_type=jnp.float32)
    txt_grad = lax.dot_general(txt_feat, txt_back, dims, preferred_element_type=jnp.float32)
    return (img_grad, txt_grad)
```

```python
import functools

import jax
import jax.numpy as jnp
from jax import lax
from jax.experimental import pallas as pl
from jax.experimental.pallas import tpu as pltpu
from jax.sharding import PartitionSpec as P

MESH = pl.DeviceIdType.MESH
BF16 = jnp.bfloat16
F32 = jnp.float32
STRIDE = 2


def up16(n):
    return -(-n // 16) * 16


def wait_bytes(ref, sem):
    pltpu.make_async_copy(ref, ref, sem).wait()


def reach(n, right):
    return n // 2 if right else (n - 1) // 2


def ring_gather(n, stride, source, target, device, send_sem, recv_sem, arrived):
    for k in range(-(-reach(n, True) // stride)):
        for right in (True, False):
            limit = reach(n, right)
            if stride * k >= limit:
                continue
            if k:
                arrived(right, stride * k)
            for j in range(1, stride + 1):
                m = stride * k + j
                if m <= limit:
                    pltpu.make_async_remote_copy(
                        src_ref=source(right, stride * k),
                        dst_ref=target(right, stride * k, m),
                        send_sem=send_sem,
                        recv_sem=recv_sem(right, m),
                        device_id=device(j if right else -j),
                        device_id_type=MESH,
                    ).start()
    for right in (True, False):
        limit = reach(n, right)
        for m in range(1, limit + 1):
            if m % stride or m == limit:
                arrived(right, m)


def ring_sum(n, stride, part, landing, device, send_sem, recv_sem, own):
    def send(right, d):
        hop = d - stride * ((d - 1) // stride)
        pltpu.make_async_remote_copy(
            src_ref=part(right, d),
            dst_ref=landing(right, d),
            send_sem=send_sem,
            recv_sem=recv_sem(right, d),
            device_id=device(hop if right else -hop),
            device_id_type=MESH,
        ).start()

    def collect(right, d, value):
        for m in range(d + 1, min(d + stride, reach(n, right)) + 1):
            ref = landing(right, m)
            wait_bytes(ref, recv_sem(right, m))
            value = value + ref[...].astype(F32)
        return value

    later = []
    for d in range(reach(n, True), 0, -1):
        for right in (True, False):
            if d > reach(n, right):
                continue
            if d % stride == 0 and d < reach(n, right):
                later.append((right, d))
            else:
                send(right, d)
    for right, d in later:
        ref = part(right, d)
        ref[...] = collect(right, d, ref[...].astype(F32)).astype(BF16)
        send(right, d)
    return collect(False, 0, collect(True, 0, own))


def kernel(
    n_loop, n_sub, n_tp,
    scale_ref, bias_ref, imgf_ref, txtf_ref, imgw_ref, txtw_ref,
    outi_ref, outt_ref,
    proj, proj_send, proj_recv, img_all, txt_all, slope,
    img_part, txt_part, img_recv, txt_recv, img_own, txt_own,
    back, back_all, feats, feat_all,
    grad, grad_part, grad_recv, pair_send, pair_recv, full,
    feat_sems, proj_sems, img_sems, txt_send, txt_gather, img_sum_sems,
    txt_sum_send, txt_sum, back_sems, grad_send, grad_sum, pair_sems,
    full_send, full_gather, core_sems,
):
    batch = imgf_ref.shape[0]
    depth, width = imgw_ref.shape
    rows = batch // n_tp
    plane = n_loop * n_tp
    pairs = batch * n_loop * n_sub
    n_hi = n_loop // 2
    loop = lax.axis_index("loop")
    z = lax.axis_index("sub")
    tp = lax.axis_index("tp")
    core = lax.rem(loop, 2)
    here = loop * n_tp + tp
    partner = (loop + 1 - 2 * core, z, tp)

    def in_plane(d):
        p = lax.rem(here + d, plane)
        return (p // n_tp, z, lax.rem(p, n_tp))

    def in_ring(d):
        return (loop, lax.rem(z + d + n_sub, n_sub), tp)

    barrier = pltpu.get_barrier_semaphore()

    def greet(d, carry):
        pl.semaphore_signal(barrier, inc=1, device_id=in_plane(d), device_id_type=MESH)
        return carry

    lax.fori_loop(1, plane, greet, 0)
    ring = sorted({d % n_sub for j in range(1, STRIDE + 1) for d in (j, -j)} - {0})
    for d in ring:
        pl.semaphore_signal(barrier, inc=1, device_id=in_ring(d), device_id_type=MESH)

    for w, (f_ref, w_ref) in enumerate(((imgf_ref, imgw_ref), (txtf_ref, txtw_ref))):
        feats[w] = f_ref[...]
        proj[w] = jnp.dot(f_ref[...], w_ref[...], preferred_element_type=F32)
        for t in range(n_tp):
            proj_send[t, w] = proj[w, t * rows:(t + 1) * rows].astype(BF16)
    pl.semaphore_wait(barrier, plane - 1 + len(ring))

    def send_proj(d, carry):
        t = lax.rem(tp + d, n_tp)
        pltpu.make_async_remote_copy(
            src_ref=proj_send.at[t], dst_ref=proj_recv.at[d - 1],
            send_sem=proj_sems.at[0], recv_sem=proj_sems.at[1],
            device_id=(loop, z, t), device_id_type=MESH,
        ).start()
        return carry

    lax.fori_loop(1, n_tp, send_proj, 0)
    mine = pl.ds(pl.multiple_of(core * batch, batch), batch)
    pltpu.make_async_remote_copy(
        src_ref=feats.at[1 - core], dst_ref=feat_all.at[mine],
        send_sem=feat_sems.at[0], recv_sem=feat_sems.at[1],
        device_id=partner, device_id_type=MESH,
    ).start()
    feat_all[mine] = feats[core]

    wait_bytes(proj_recv.at[pl.ds(0, n_tp - 1)], proj_sems.at[1])
    units, inverses = [], []
    for w in range(2):
        total = proj[w, pl.ds(pl.multiple_of(tp * rows, rows), rows)]
        for d in range(n_tp - 1):
            total = total + proj_recv[d, w].astype(F32)
        inverse = lax.rsqrt(jnp.sum(total * total, axis=-1, keepdims=True) + 1e-06)
        units.append(total * inverse)
        inverses.append(inverse)
        (img_all, txt_all)[w][0:rows] = units[w].astype(BF16)

    def slot(i):
        return pl.ds(i * rows, rows)

    def back_slot(right, m):
        return m if right else (n_sub - m) % n_sub

    def send_img(d, carry):
        pltpu.make_async_remote_copy(
            src_ref=img_all.at[0:rows],
            dst_ref=img_all.at[pl.ds(pl.multiple_of(d * rows, rows), rows)],
            send_sem=img_sems.at[0], recv_sem=img_sems.at[1],
            device_id=in_plane(d), device_id_type=MESH,
        ).start()
        return carry

    lax.fori_loop(1, plane, send_img, 0)

    def txt_arrived(right, m):
        s = back_slot(right, m)
        wait_bytes(txt_all.at[slot(s)], txt_gather.at[s])

    ring_gather(
        n_sub, STRIDE,
        source=lambda right, m: txt_all.at[slot(back_slot(right, m))],
        target=lambda right, m, m2: txt_all.at[slot(back_slot(right, m2))],
        device=in_ring, send_sem=txt_send,
        recv_sem=lambda right, m: txt_gather.at[back_slot(right, m)],
        arrived=txt_arrived,
    )
    wait_bytes(img_all.at[rows:plane * rows], img_sems.at[1])

    scale = scale_ref[0]
    bias = bias_ref[0]
    n_img, n_txt = plane * rows, n_sub * rows
    step = min(128, n_img)
    for i in range(0, n_img, step):
        logits = scale * lax.dot_general(
            img_all[i:i + step], txt_all[...], (((1,), (1,)), ((), ())),
            preferred_element_type=F32,
        ) + bias
        value = jax.nn.sigmoid(logits)
        if i < rows:
            r = lax.broadcasted_iota(jnp.int32, logits.shape, 0) + i
            c = lax.broadcasted_iota(jnp.int32, logits.shape, 1)
            value = value - jnp.where((r == c) & (r < rows), 1.0, 0.0)
        slope[i:i + step] = (scale * value / pairs).astype(BF16)
        d_img = jnp.dot(slope[i:i + step], txt_all[...], preferred_element_type=F32)
        if i == 0:
            img_own[...] = d_img[0:rows]
        img_part[i:i + step] = d_img.astype(BF16)
    step = min(128, n_txt)
    for i in range(0, n_txt, step):
        d_txt = lax.dot_general(
            slope[:, i:i + step], img_all[...], (((0,), (0,)), ((), ())),
            preferred_element_type=F32,
        )
        if i == 0:
            txt_own[...] = d_txt[0:rows]
        txt_part[i:i + step] = d_txt.astype(BF16)

    def send_img_part(d, carry):
        pltpu.make_async_remote_copy(
            src_ref=img_part.at[pl.ds(pl.multiple_of(d * rows, rows), rows)],
            dst_ref=img_recv.at[pl.ds(pl.multiple_of((d - 1) * rows, rows), rows)],
            send_sem=img_sum_sems.at[0], recv_sem=img_sum_sems.at[1],
            device_id=in_plane(plane - d), device_id_type=MESH,
        ).start()
        return carry

    lax.fori_loop(1, plane, send_img_part, 0)

    def lane(right, m):
        return m if right else n_sub - m

    d_txt = ring_sum(
        n_sub, STRIDE,
        part=lambda right, d: txt_part.at[slot((n_sub - d) if right else d)],
        landing=lambda right, d: txt_recv.at[slot(lane(right, d))],
        device=in_ring, send_sem=txt_sum_send,
        recv_sem=lambda right, d: txt_sum.at[lane(right, d)],
        own=txt_own[...],
    )
    wait_bytes(img_recv.at[0:(plane - 1) * rows], img_sum_sems.at[1])
    d_img = img_own[...]
    for d in range(plane - 1):
        d_img = d_img + img_recv[d * rows:(d + 1) * rows].astype(F32)
    for w, upstream in enumerate((d_img, d_txt)):
        inner = jnp.sum(units[w] * upstream, axis=-1, keepdims=True)
        back[w] = ((upstream - units[w] * inner) * inverses[w]).astype(BF16)

    spot = pl.ds(pl.multiple_of((core * n_tp + tp) * rows, rows), rows)

    def send_back(d, carry):
        t = lax.rem(tp + d, n_tp)
        for w in range(2):
            pltpu.make_async_remote_copy(
                src_ref=back.at[w], dst_ref=back_all.at[spot],
                send_sem=back_sems.at[0], recv_sem=back_sems.at[1],
                device_id=(loop - core + w, z, t), device_id_type=MESH,
            ).start()
        return carry

    lax.fori_loop(1, n_tp, send_back, 0)
    pltpu.make_async_remote_copy(
        src_ref=back.at[1 - core], dst_ref=back_all.at[spot],
        send_sem=back_sems.at[0], recv_sem=back_sems.at[1],
        device_id=partner, device_id_type=MESH,
    ).start()
    back_all[spot] = back[core]
    wait_bytes(feat_all.at[0:batch], feat_sems.at[1])
    wait_bytes(back_all.at[0:(2 * n_tp - 1) * rows], back_sems.at[1])

    total = lax.dot_general(
        feat_all[...], back_all[...], (((0,), (0,)), ((), ())), preferred_element_type=F32
    )
    for k in range(width // 128):
        grad[k * depth:(k + 1) * depth] = total[:, k * 128:(k + 1) * 128]
    used = width // 128 * depth
    if used < grad.shape[0]:
        grad[used:] = jnp.zeros((grad.shape[0] - used, 128), F32)
    grad_part[...] = grad[...].astype(BF16)
    chunk = grad.shape[0] // n_sub

    def piece(owner):
        return pl.ds(pl.multiple_of(lax.rem(owner + n_sub, n_sub) * chunk, chunk), chunk)

    mean = ring_sum(
        n_sub, STRIDE,
        part=lambda right, d: grad_part.at[piece(z + d if right else z - d)],
        landing=lambda right, d: grad_recv.at[lane(right, d)],
        device=in_ring, send_sem=grad_send,
        recv_sem=lambda right, d: grad_sum.at[lane(right, d)],
        own=grad[piece(z)],
    )
    if n_hi > 1:
        pair_send[...] = mean
        pltpu.make_async_remote_copy(
            src_ref=pair_send, dst_ref=pair_recv,
            send_sem=pair_sems.at[0], recv_sem=pair_sems.at[1],
            device_id=(lax.rem(loop + 2, n_loop), z, tp), device_id_type=MESH,
        ).start()
        wait_bytes(pair_recv, pair_sems.at[1])
        mean = mean + pair_recv[...]
    whole = full.at[core]
    full[core, piece(z)] = mean.astype(BF16)

    def origin(right, m):
        return full.at[core, piece(z - m if right else z + m)]

    def full_arrived(right, m):
        wait_bytes(origin(right, m), full_gather.at[lane(right, m)])

    ring_gather(
        n_sub, STRIDE,
        source=origin,
        target=lambda right, m, m2: origin(right, m),
        device=in_ring, send_sem=full_send,
        recv_sem=lambda right, m: full_gather.at[lane(right, m)],
        arrived=full_arrived,
    )
    pltpu.make_async_remote_copy(
        src_ref=whole, dst_ref=whole,
        send_sem=core_sems.at[0], recv_sem=core_sems.at[1],
        device_id=partner, device_id_type=MESH,
    ).start()
    wait_bytes(full.at[1 - core], core_sems.at[1])
    for w, out_ref in enumerate((outi_ref, outt_ref)):
        for k in range(width // 128):
            out_ref[:, k * 128:(k + 1) * 128] = full[w, k * depth:(k + 1) * depth].astype(F32)

    wait_bytes(proj_send.at[pl.ds(0, n_tp - 1)], proj_sems.at[0])
    wait_bytes(feat_all.at[0:batch], feat_sems.at[0])
    wait_bytes(img_all.at[rows:plane * rows], img_sems.at[0])
    wait_bytes(txt_all.at[rows:n_sub * rows], txt_send)
    wait_bytes(img_recv.at[0:(plane - 1) * rows], img_sum_sems.at[0])
    wait_bytes(txt_all.at[rows:n_sub * rows], txt_sum_send)
    wait_bytes(back_all.at[0:(2 * n_tp - 1) * rows], back_sems.at[0])
    wait_bytes(grad_part.at[chunk:n_sub * chunk], grad_send)
    if n_hi > 1:
        wait_bytes(pair_send, pair_sems.at[0])
    wait_bytes(grad_part.at[chunk:n_sub * chunk], full_send)
    wait_bytes(whole, core_sems.at[0])


def per_device(n_loop, n_sub, n_tp, img_feat, txt_feat, img_weight, txt_weight, scale, bias):
    batch = img_feat.shape[0]
    depth, width = img_weight.shape
    rows = batch // n_tp
    plane = n_loop * n_tp
    n_img, n_txt = plane * rows, n_sub * rows
    chunk = up16(-(-width // 128 * depth // n_sub))
    dma = pltpu.SemaphoreType.DMA
    vmem = pl.BlockSpec(memory_space=pltpu.VMEM)
    smem = pl.BlockSpec(memory_space=pltpu.SMEM)
    out = jax.ShapeDtypeStruct((depth, width), F32)
    return pl.pallas_call(
        functools.partial(kernel, n_loop, n_sub, n_tp),
        out_shape=(out, out),
        in_specs=[smem, smem] + [vmem] * 4,
        out_specs=(vmem, vmem),
        scratch_shapes=[
            pltpu.VMEM((2, batch, width), F32),
            pltpu.VMEM((n_tp, 2, rows, width), BF16),
            pltpu.VMEM((n_tp, 2, rows, width), BF16),
            pltpu.VMEM((n_img, width), BF16),
            pltpu.VMEM((n_txt, width), BF16),
            pltpu.VMEM((n_img, n_txt), BF16),
            pltpu.VMEM((n_img, width), BF16),
            pltpu.VMEM((n_txt, width), BF16),
            pltpu.VMEM((n_img, width), BF16),
            pltpu.VMEM((n_txt, width), BF16),
            pltpu.VMEM((rows, width), F32),
            pltpu.VMEM((rows, width), F32),
            pltpu.VMEM((2, rows, width), BF16),
            pltpu.VMEM((2 * n_tp * rows, width), BF16),
            pltpu.VMEM((2, batch, depth), BF16),
            pltpu.VMEM((2 * batch, depth), BF16),
            pltpu.VMEM((n_sub * chunk, 128), F32),
            pltpu.VMEM((n_sub * chunk, 128), BF16),
            pltpu.VMEM((n_sub, chunk, 128), BF16),
            pltpu.VMEM((chunk, 128), F32),
            pltpu.VMEM((chunk, 128), F32),
            pltpu.VMEM((2, n_sub * chunk, 128), BF16),
            dma((2,)),
            dma((2,)),
            dma((2,)),
            dma,
            dma((n_sub,)),
            dma((2,)),
            dma,
            dma((n_sub,)),
            dma((2,)),
            dma,
            dma((n_sub,)),
            dma((2,)),
            dma,
            dma((n_sub,)),
            dma((2,)),
        ],
        compiler_params=pltpu.CompilerParams(
            collective_id=0, has_side_effects=True, vmem_limit_bytes=48 * 1024 * 1024
        ),
        cost_estimate=pl.CostEstimate(
            flops=6 * n_img * n_txt * width, bytes_accessed=4 * depth * width * 3, transcendentals=0
        ),
    )(scale, bias, img_feat, txt_feat, img_weight, txt_weight)


def solution(mesh):
    placed = (
        P(("loop", "sub"), "tp"),
        P(("loop", "sub"), "tp"),
        P("tp", None),
        P("tp", None),
        P(),
        P(),
    )
    sizes = (mesh.shape["loop"], mesh.shape["sub"], mesh.shape["tp"])
    return jax.shard_map(
        functools.partial(per_device, *sizes),
        mesh=mesh,
        in_specs=placed,
        out_specs=(P("tp", None), P("tp", None)),
        check_vma=False,
    )
```

```python
import functools

import jax
import jax.numpy as jnp
from jax import lax
from jax.experimental import pallas as pl
from jax.experimental.pallas import tpu as pltpu
from jax.sharding import PartitionSpec as P

MESH = pl.DeviceIdType.MESH
BF16 = jnp.bfloat16
F32 = jnp.float32
STRIDE = 3
ALL_RING = False


def up16(n):
    return -(-n // 16) * 16


def wait_bytes(ref, sem):
    pltpu.make_async_copy(ref, ref, sem).wait()


def reach(n, right):
    return n // 2 if right else (n - 1) // 2


def ring_sends(n, stride, k, source, target, device, send_sem, recv_sem):
    for right in (True, False):
        for j in range(stride, 0, -1):
            m = stride * k + j
            if m <= reach(n, right):
                pltpu.make_async_remote_copy(
                    src_ref=source(right, stride * k),
                    dst_ref=target(right, m),
                    send_sem=send_sem,
                    recv_sem=recv_sem(right, m),
                    device_id=device(j if right else -j),
                    device_id_type=MESH,
                ).start()


def ring_sum(n, stride, part, landing, device, send_sem, recv_sem, between):
    def send(right, d):
        hop = d - stride * ((d - 1) // stride)
        pltpu.make_async_remote_copy(
            src_ref=part(right, d),
            dst_ref=landing(right, d),
            send_sem=send_sem,
            recv_sem=recv_sem(right, d),
            device_id=device(hop if right else -hop),
            device_id_type=MESH,
        ).start()

    def collect(right, d, value):
        for m in range(d + 1, min(d + stride, reach(n, right)) + 1):
            ref = landing(right, m)
            wait_bytes(ref, recv_sem(right, m))
            value = value + ref[...].astype(F32)
        return value

    later = []
    for d in range(reach(n, True), 0, -1):
        for right in (True, False):
            if d > reach(n, right):
                continue
            if d % stride == 0 and d < reach(n, right):
                later.append((right, d))
            else:
                send(right, d)
    steps = sorted({d for _, d in later}, reverse=True)
    for at, d in enumerate(steps + [0]):
        between(at, len(steps))
        for right in (True, False):
            if (right, d) in later:
                ref = part(right, d)
                ref[...] = collect(right, d, ref[...].astype(F32)).astype(BF16)
                send(right, d)
    return collect(False, 0, collect(True, 0, jnp.zeros(part(True, 0).shape, F32)))


def kernel(
    n_loop, n_sub, n_tp,
    scale_ref, bias_ref, imgf_hbm, txtf_hbm, imgw_hbm, txtw_hbm,
    outi_ref, outt_ref,
    feats, weights, proj, proj_send, proj_recv, img_all, txt_all, slope,
    img_part, txt_part, img_pair, img_recv, txt_recv, img_own, txt_own,
    back, back_all, feat_all,
    grad, half_send, half_recv, grad_part, grad_recv, full, ordered,
    load_sems, feat_sems, proj_sems, img_send, img_gather, img_core, txt_send, txt_gather,
    img_sum_sems, img_pair_sems, txt_sum_send, txt_sum, back_sems, half_sems, grad_sems,
    full_send, full_gather, hi_send, hi_gather, core_sems,
):
    _, batch, depth = feats.shape
    width = weights.shape[2]
    rows = batch // n_tp
    n_hi = n_loop // 2
    chips = n_hi * n_tp
    pairs = batch * n_loop * n_sub
    loop = lax.axis_index("loop")
    z = lax.axis_index("sub")
    tp = lax.axis_index("tp")
    core = lax.rem(loop, 2)
    hi = loop // 2
    chip = hi * n_tp + tp
    partner = (loop + 1 - 2 * core, z, tp)
    across = (lax.rem(loop + 2, n_loop), z, tp)

    def in_plane(d):
        p = lax.rem(chip + d, chips)
        return (p // n_tp * 2 + core, z, lax.rem(p, n_tp))

    def in_ring(d):
        return (loop, lax.rem(z + d + n_sub, n_sub), tp)

    def greet(device):
        pl.semaphore_signal(barrier, inc=1, device_id=device, device_id_type=MESH)

    barrier = pltpu.get_barrier_semaphore()
    ring = sorted({d % n_sub for j in range(1, STRIDE + 1) for d in (j, -j)} - {0})
    if ALL_RING:
        ring = list(range(1, n_sub))
    for d in ring:
        greet(in_ring(d))
    for d in range(1, chips):
        greet(in_plane(d))
    greet(partner)
    for d in range(1, n_tp):
        greet((loop + 1 - 2 * core, z, lax.rem(tp + d, n_tp)))
    greeted = len(ring) + chips - 1 + 1 + n_tp - 1

    loads = []
    for w, (f_hbm, w_hbm) in ((1, (txtf_hbm, txtw_hbm)), (0, (imgf_hbm, imgw_hbm))):
        for i, (src, dst) in enumerate(((f_hbm, feats.at[w]), (w_hbm, weights.at[w]))):
            load = pltpu.make_async_copy(src, dst, load_sems.at[w, i])
            load.start()
            loads.append(load)
    for at, w in enumerate((1, 0)):
        loads[2 * at].wait()
        loads[2 * at + 1].wait()
        proj[w] = jnp.dot(feats[w], weights[w], preferred_element_type=F32)
        for t in range(n_tp):
            proj_send[w, t] = proj[w, t * rows:(t + 1) * rows].astype(BF16)
    pl.semaphore_wait(barrier, greeted)
    for w in (1, 0):
        for d in range(1, n_tp):
            t = lax.rem(tp + d, n_tp)
            pltpu.make_async_remote_copy(
                src_ref=proj_send.at[w, t], dst_ref=proj_recv.at[w, d - 1],
                send_sem=proj_sems.at[w, 0], recv_sem=proj_sems.at[w, 1],
                device_id=(loop, z, t), device_id_type=MESH,
            ).start()
    mine = pl.ds(pl.multiple_of(core * batch, batch), batch)
    pltpu.make_async_remote_copy(
        src_ref=feats.at[1 - core], dst_ref=feat_all.at[mine],
        send_sem=feat_sems.at[0], recv_sem=feat_sems.at[1],
        device_id=partner, device_id_type=MESH,
    ).start()
    feat_all[mine] = feats[core]

    def embed(w):
        wait_bytes(proj_recv.at[w, pl.ds(0, n_tp - 1)], proj_sems.at[w, 1])
        total = proj[w, pl.ds(pl.multiple_of(tp * rows, rows), rows)]
        for d in range(n_tp - 1):
            total = total + proj_recv[w, d].astype(F32)
        inverse = lax.rsqrt(jnp.sum(total * total, axis=-1, keepdims=True) + 1e-06)
        unit = total * inverse
        (img_all, txt_all)[w][0:rows] = unit.astype(BF16)
        return unit, inverse

    def slot(i):
        return pl.ds(i * rows, rows)

    def lane(right, m):
        return m if right else (n_sub - m) % n_sub

    def send_txt(k):
        ring_sends(
            n_sub, STRIDE, k,
            source=lambda right, m: txt_all.at[slot(lane(right, m))],
            target=lambda right, m: txt_all.at[slot(lane(right, m))],
            device=in_ring, send_sem=txt_send,
            recv_sem=lambda right, m: txt_gather.at[lane(right, m)],
        )

    def txt_arrived(right, m):
        wait_bytes(txt_all.at[slot(lane(right, m))], txt_gather.at[lane(right, m)])

    txt_unit, txt_inverse = embed(1)
    send_txt(0)
    img_unit, img_inverse = embed(0)
    for d in range(1, chips):
        pltpu.make_async_remote_copy(
            src_ref=img_all.at[slot(0)], dst_ref=img_all.at[slot(d)],
            send_sem=img_send, recv_sem=img_gather.at[d],
            device_id=in_plane(d), device_id_type=MESH,
        ).start()
    half_img = chips * rows
    group = max(1, chips // 4)

    def forward_img():
        for g in range(0, chips, group):
            for d in range(max(g, 1), g + group):
                wait_bytes(img_all.at[slot(d)], img_gather.at[d])
            pltpu.make_async_remote_copy(
                src_ref=img_all.at[g * rows:(g + group) * rows],
                dst_ref=img_all.at[half_img + g * rows:half_img + (g + group) * rows],
                send_sem=img_core.at[0], recv_sem=img_core.at[1],
                device_id=partner, device_id_type=MESH,
            ).start()

    steps = -(-reach(n_sub, True) // STRIDE)
    for k in range(1, steps):
        if k == steps - 1:
            forward_img()
        for right in (True, False):
            if STRIDE * k < reach(n_sub, right):
                txt_arrived(right, STRIDE * k)
        send_txt(k)
    if steps == 1:
        forward_img()
    for right in (True, False):
        for m in range(1, reach(n_sub, right) + 1):
            if m % STRIDE or m == reach(n_sub, right):
                txt_arrived(right, m)
    wait_bytes(img_all.at[half_img:2 * half_img], img_core.at[1])

    scale = scale_ref[0]
    bias = bias_ref[0]
    n_img, n_txt = 2 * half_img, n_sub * rows
    step = min(128, half_img)
    for i in range(0, n_img, step):
        logits = scale * lax.dot_general(
            img_all[i:i + step], txt_all[...], (((1,), (1,)), ((), ())),
            preferred_element_type=F32,
        ) + bias
        value = jax.nn.sigmoid(logits)
        if i < rows:
            r = lax.broadcasted_iota(jnp.int32, logits.shape, 0) + i
            c = lax.broadcasted_iota(jnp.int32, logits.shape, 1)
            value = value - jnp.where((r == c) & (r < rows), 1.0, 0.0)
        slope[i:i + step] = (scale * value / pairs).astype(BF16)
    width_txt = min(128, n_txt)
    for i in range(0, n_txt, width_txt):
        d_txt = lax.dot_general(
            slope[:, i:i + width_txt], img_all[...], (((0,), (0,)), ((), ())),
            preferred_element_type=F32,
        )
        if i == 0:
            txt_own[...] = d_txt[0:rows]
        txt_part[i:i + width_txt] = d_txt.astype(BF16)

    def img_grad(start):
        for i in range(start, start + half_img, step):
            d_img = jnp.dot(slope[i:i + step], txt_all[...], preferred_element_type=F32)
            if i == 0:
                img_own[...] = d_img[0:rows]
            img_part[i:i + step] = d_img.astype(BF16)

    def share_img():
        img_grad(half_img)
        pltpu.make_async_remote_copy(
            src_ref=img_part.at[half_img:n_img], dst_ref=img_pair,
            send_sem=img_pair_sems.at[0], recv_sem=img_pair_sems.at[1],
            device_id=partner, device_id_type=MESH,
        ).start()
        img_grad(0)
        wait_bytes(img_pair, img_pair_sems.at[1])
        for d in range(1, chips):
            img_part[slot(d)] = (
                img_part[slot(d)].astype(F32) + img_pair[slot(d)].astype(F32)
            ).astype(BF16)
            pltpu.make_async_remote_copy(
                src_ref=img_part.at[slot(d)], dst_ref=img_recv.at[slot(d - 1)],
                send_sem=img_sum_sems.at[0], recv_sem=img_sum_sems.at[1],
                device_id=in_plane(chips - d), device_id_type=MESH,
            ).start()

    spot = pl.ds(pl.multiple_of((core * n_tp + tp) * rows, rows), rows)

    def send_back(w, unit, inverse, upstream):
        inner = jnp.sum(unit * upstream, axis=-1, keepdims=True)
        back[w] = ((upstream - unit * inner) * inverse).astype(BF16)
        for d in range(1, n_tp):
            pltpu.make_async_remote_copy(
                src_ref=back.at[w], dst_ref=back_all.at[spot],
                send_sem=back_sems.at[0], recv_sem=back_sems.at[1],
                device_id=(loop - core + w, z, lax.rem(tp + d, n_tp)), device_id_type=MESH,
            ).start()

    def finish_img():
        wait_bytes(img_recv.at[0:(chips - 1) * rows], img_sum_sems.at[1])
        d_img = img_own[...] + img_pair[slot(0)].astype(F32)
        for d in range(chips - 1):
            d_img = d_img + img_recv[slot(d)].astype(F32)
        send_back(0, img_unit, img_inverse, d_img)

    def between(at, last):
        if at == 0:
            share_img()
        if at == last:
            finish_img()

    d_txt = txt_own[...] + ring_sum(
        n_sub, STRIDE,
        part=lambda right, d: txt_part.at[slot(lane(not right, d))],
        landing=lambda right, d: txt_recv.at[slot(lane(right, d))],
        device=in_ring, send_sem=txt_sum_send,
        recv_sem=lambda right, d: txt_sum.at[lane(right, d)],
        between=between,
    )
    send_back(1, txt_unit, txt_inverse, d_txt)
    pltpu.make_async_remote_copy(
        src_ref=back.at[1 - core], dst_ref=back_all.at[spot],
        send_sem=back_sems.at[0], recv_sem=back_sems.at[1],
        device_id=partner, device_id_type=MESH,
    ).start()
    back_all[spot] = back[core]
    wait_bytes(feat_all.at[0:batch], feat_sems.at[1])
    wait_bytes(back_all.at[0:(2 * n_tp - 1) * rows], back_sems.at[1])

    total = lax.dot_general(
        feat_all[...], back_all[...], (((0,), (0,)), ((), ())), preferred_element_type=F32
    )
    half = depth // 2
    tiles = width // 128
    for h in range(2):
        for k in range(tiles):
            grad[h, k * half:(k + 1) * half] = (
                total[h * half:(h + 1) * half, k * 128:(k + 1) * 128]
            )
        if tiles * half < grad.shape[1]:
            grad[h, tiles * half:] = jnp.zeros((grad.shape[1] - tiles * half, 128), F32)
    sent = half_send.shape[0]
    half_send[...] = grad[1 - hi, 0:sent].astype(BF16)
    pltpu.make_async_remote_copy(
        src_ref=half_send, dst_ref=half_recv,
        send_sem=half_sems.at[0], recv_sem=half_sems.at[1],
        device_id=across, device_id_type=MESH,
    ).start()
    wait_bytes(half_recv, half_sems.at[1])
    grad[hi, 0:sent] = grad[hi, 0:sent] + half_recv[...].astype(F32)
    grad_part[...] = grad[hi].astype(BF16)
    chunk = grad.shape[1] // n_sub

    def piece(owner):
        return pl.ds(pl.multiple_of(lax.rem(owner + n_sub, n_sub) * chunk, chunk), chunk)

    def tile_slot(i):
        return pl.ds(i * chunk, chunk)

    far_first = sorted(range(1, n_sub), key=lambda d: (-min(d, n_sub - d), d))
    for d in far_first:
        pltpu.make_async_remote_copy(
            src_ref=grad_part.at[piece(z + d)], dst_ref=grad_recv.at[d - 1],
            send_sem=grad_sems.at[0], recv_sem=grad_sems.at[1],
            device_id=in_ring(d), device_id_type=MESH,
        ).start()
    done = grad[hi, piece(z)]
    wait_bytes(grad_recv, grad_sems.at[1])
    for d in range(n_sub - 1):
        done = done + grad_recv[d].astype(F32)
    held = full.at[core, hi]
    other = full.at[core, 1 - hi]
    full[core, hi, 0:chunk] = done.astype(BF16)
    for d in far_first:
        pltpu.make_async_remote_copy(
            src_ref=held.at[tile_slot(0)], dst_ref=held.at[tile_slot(d)],
            send_sem=full_send, recv_sem=full_gather.at[d],
            device_id=in_ring(d), device_id_type=MESH,
        ).start()
    per = max(1, n_sub // 4)
    starts = list(range(0, n_sub, per))
    starts.sort(key=lambda s: min(s + per - 1, n_sub - s))

    def to_core(ref):
        pltpu.make_async_remote_copy(
            src_ref=ref, dst_ref=ref, send_sem=core_sems.at[0], recv_sem=core_sems.at[1],
            device_id=partner, device_id_type=MESH,
        ).start()

    for g, s in enumerate(starts):
        for d in range(max(s, 1), s + per):
            wait_bytes(held.at[tile_slot(d)], full_gather.at[d])
        ref = held.at[s * chunk:(s + per) * chunk]
        pltpu.make_async_remote_copy(
            src_ref=ref, dst_ref=ref, send_sem=hi_send, recv_sem=hi_gather.at[g],
            device_id=across, device_id_type=MESH,
        ).start()
        to_core(ref)
    for g, s in enumerate(starts):
        ref = other.at[s * chunk:(s + per) * chunk]
        wait_bytes(ref, hi_gather.at[g])
        to_core(ref)
    wait_bytes(full.at[1 - core], core_sems.at[1])
    for w, out_ref in enumerate((outi_ref, outt_ref)):
        for h in range(2):
            for d in range(n_sub):
                ordered[piece(z - d)] = full[w, h, tile_slot(d)].astype(F32)
            for k in range(tiles):
                out_ref[h * half:(h + 1) * half, k * 128:(k + 1) * 128] = (
                    ordered[k * half:(k + 1) * half]
                )

    for w in range(2):
        wait_bytes(proj_send.at[w, pl.ds(0, n_tp - 1)], proj_sems.at[w, 0])
    wait_bytes(feat_all.at[0:batch], feat_sems.at[0])
    wait_bytes(img_all.at[rows:half_img], img_send)
    wait_bytes(img_all.at[0:half_img], img_core.at[0])
    wait_bytes(txt_all.at[rows:n_txt], txt_send)
    wait_bytes(img_pair, img_pair_sems.at[0])
    wait_bytes(img_recv.at[0:(chips - 1) * rows], img_sum_sems.at[0])
    wait_bytes(txt_all.at[rows:n_txt], txt_sum_send)
    wait_bytes(back_all.at[0:(2 * n_tp - 1) * rows], back_sems.at[0])
    wait_bytes(half_send, half_sems.at[0])
    wait_bytes(grad_recv, grad_sems.at[0])
    wait_bytes(held.at[chunk:n_sub * chunk], full_send)
    wait_bytes(held, hi_send)
    wait_bytes(full.at[core], core_sems.at[0])


def per_device(n_loop, n_sub, n_tp, img_feat, txt_feat, img_weight, txt_weight, scale, bias):
    batch = img_feat.shape[0]
    depth, width = img_weight.shape
    rows = batch // n_tp
    half_img, n_txt = n_loop // 2 * n_tp * rows, n_sub * rows
    n_img = 2 * half_img
    used = width // 128 * depth // 2
    chunk = up16(-(-used // n_sub))
    dma = pltpu.SemaphoreType.DMA
    vmem = pl.BlockSpec(memory_space=pltpu.VMEM)
    smem = pl.BlockSpec(memory_space=pltpu.SMEM)
    out = jax.ShapeDtypeStruct((depth, width), F32)
    return pl.pallas_call(
        functools.partial(kernel, n_loop, n_sub, n_tp),
        out_shape=(out, out),
        in_specs=[smem, smem] + [pl.BlockSpec(memory_space=pl.ANY)] * 4,
        out_specs=(vmem, vmem),
        scratch_shapes=[
            pltpu.VMEM((2, batch, depth), BF16),
            pltpu.VMEM((2, depth, width), BF16),
            pltpu.VMEM((2, batch, width), F32),
            pltpu.VMEM((2, n_tp, rows, width), BF16),
            pltpu.VMEM((2, n_tp - 1, rows, width), BF16),
            pltpu.VMEM((n_img, width), BF16),
            pltpu.VMEM((n_txt, width), BF16),
            pltpu.VMEM((n_img, n_txt), BF16),
            pltpu.VMEM((n_img, width), BF16),
            pltpu.VMEM((n_txt, width), BF16),
            pltpu.VMEM((half_img, width), BF16),
            pltpu.VMEM((half_img, width), BF16),
            pltpu.VMEM((n_txt, width), BF16),
            pltpu.VMEM((rows, width), F32),
            pltpu.VMEM((rows, width), F32),
            pltpu.VMEM((2, rows, width), BF16),
            pltpu.VMEM((2 * n_tp * rows, width), BF16),
            pltpu.VMEM((2 * batch, depth), BF16),
            pltpu.VMEM((2, n_sub * chunk, 128), F32),
            pltpu.VMEM((up16(used), 128), BF16),
            pltpu.VMEM((up16(used), 128), BF16),
            pltpu.VMEM((n_sub * chunk, 128), BF16),
            pltpu.VMEM((n_sub - 1, chunk, 128), BF16),
            pltpu.VMEM((2, 2, n_sub * chunk, 128), BF16),
            pltpu.VMEM((n_sub * chunk, 128), F32),
            dma((2, 2)),
            dma((2,)),
            dma((2, 2)),
            dma,
            dma((n_loop // 2 * n_tp,)),
            dma((2,)),
            dma,
            dma((n_sub,)),
            dma((2,)),
            dma((2,)),
            dma,
            dma((n_sub,)),
            dma((2,)),
            dma((2,)),
            dma((2,)),
            dma,
            dma((n_sub,)),
            dma,
            dma((4,)),
            dma((2,)),
        ],
        compiler_params=pltpu.CompilerParams(
            collective_id=0, has_side_effects=True, vmem_limit_bytes=48 * 1024 * 1024
        ),
        cost_estimate=pl.CostEstimate(
            flops=6 * n_img * n_txt * width, bytes_accessed=4 * depth * width * 3, transcendentals=0
        ),
    )(scale, bias, img_feat, txt_feat, img_weight, txt_weight)


def solution(mesh):
    placed = (
        P(("loop", "sub"), "tp"),
        P(("loop", "sub"), "tp"),
        P("tp", None),
        P("tp", None),
        P(),
        P(),
    )
    sizes = (mesh.shape["loop"], mesh.shape["sub"], mesh.shape["tp"])
    return jax.shard_map(
        functools.partial(per_device, *sizes),
        mesh=mesh,
        in_specs=placed,
        out_specs=(P("tp", None), P("tp", None)),
        check_vma=False,
    )
```

```python
import functools

import jax
import jax.numpy as jnp
from jax import lax
from jax.experimental import pallas as pl
from jax.experimental.pallas import tpu as pltpu
from jax.sharding import PartitionSpec as P

MESH = pl.DeviceIdType.MESH
BF16 = jnp.bfloat16
F32 = jnp.float32
STRIDE = 3
FULL_STRIDE = 4


def up16(n):
    return -(-n // 16) * 16


def wait_bytes(ref, sem):
    pltpu.make_async_copy(ref, ref, sem).wait()


def reach(n, right):
    return n // 2 if right else (n - 1) // 2


def ring_sends(n, stride, k, source, target, device, send_sem, recv_sem):
    for right in (True, False):
        for j in range(stride, 0, -1):
            m = stride * k + j
            if m <= reach(n, right):
                pltpu.make_async_remote_copy(
                    src_ref=source(right, stride * k),
                    dst_ref=target(right, m),
                    send_sem=send_sem,
                    recv_sem=recv_sem(right, m),
                    device_id=device(j if right else -j),
                    device_id_type=MESH,
                ).start()


def ring_sum(n, stride, part, landing, device, send_sem, recv_sem, between):
    def send(right, d):
        hop = d - stride * ((d - 1) // stride)
        pltpu.make_async_remote_copy(
            src_ref=part(right, d),
            dst_ref=landing(right, d),
            send_sem=send_sem,
            recv_sem=recv_sem(right, d),
            device_id=device(hop if right else -hop),
            device_id_type=MESH,
        ).start()

    def collect(right, d, value):
        for m in range(d + 1, min(d + stride, reach(n, right)) + 1):
            ref = landing(right, m)
            wait_bytes(ref, recv_sem(right, m))
            value = value + ref[...].astype(F32)
        return value

    later = []
    for d in range(reach(n, True), 0, -1):
        for right in (True, False):
            if d > reach(n, right):
                continue
            if d % stride == 0 and d < reach(n, right):
                later.append((right, d))
            else:
                send(right, d)
    steps = sorted({d for _, d in later}, reverse=True)
    for at, d in enumerate(steps + [0]):
        between(at, len(steps))
        for right in (True, False):
            if (right, d) in later:
                ref = part(right, d)
                ref[...] = collect(right, d, ref[...].astype(F32)).astype(BF16)
                send(right, d)
    return collect(False, 0, collect(True, 0, jnp.zeros(part(True, 0).shape, F32)))


def kernel(
    n_loop, n_sub, n_tp,
    scale_ref, bias_ref, imgf_hbm, txtf_hbm, imgw_hbm, txtw_hbm,
    full_out,
    feats, weights, proj, proj_send, proj_recv, img_all, txt_all, slope,
    img_part, txt_part, img_pair, img_recv, txt_recv, img_own, txt_own,
    back, back_all, feat_all,
    both, grad, grad_part, grad_recv, full,
    load_sems, feat_sems, proj_sems, img_send, img_gather, img_core, txt_send, txt_gather,
    img_sum_sems, img_pair_sems, txt_sum_send, txt_sum, back_sems, grad_sems,
    full_send, full_gather, hi_send, hi_gather, core_sems, store_sem,
):
    _, depth, batch = feats.shape
    width = weights.shape[2]
    rows = batch // n_tp
    n_hi = n_loop // 2
    chips = n_hi * n_tp
    pairs = batch * n_loop * n_sub
    loop = lax.axis_index("loop")
    z = lax.axis_index("sub")
    tp = lax.axis_index("tp")
    core = lax.rem(loop, 2)
    hi = loop // 2
    chip = hi * n_tp + tp
    partner = (loop + 1 - 2 * core, z, tp)
    across = (lax.rem(loop + 2, n_loop), z, tp)

    def in_plane(d, to_core):
        p = lax.rem(chip + d, chips)
        return (p // n_tp * 2 + to_core, z, lax.rem(p, n_tp))

    def in_ring(d):
        return (loop, lax.rem(z + d + n_sub, n_sub), tp)

    def greet(device):
        pl.semaphore_signal(barrier, inc=1, device_id=device, device_id_type=MESH)

    barrier = pltpu.get_barrier_semaphore()
    ring = sorted({d % n_sub for j in range(1, STRIDE + 1) for d in (j, -j)} - {0})
    for d in ring:
        greet(in_ring(d))
    for d in range(1, chips):
        greet(in_plane(d, core))
    greet(partner)
    for d in range(1, chips):
        greet(in_plane(d, 1 - core))
    greeted = len(ring) + 2 * chips - 1

    loads = []
    for w, (f_hbm, w_hbm) in ((1, (txtf_hbm, txtw_hbm)), (0, (imgf_hbm, imgw_hbm))):
        for i, (src, dst) in enumerate(((f_hbm, feats.at[w]), (w_hbm, weights.at[w]))):
            load = pltpu.make_async_copy(src, dst, load_sems.at[w, i])
            load.start()
            loads.append(load)
    for at, w in enumerate((1, 0)):
        loads[2 * at].wait()
        loads[2 * at + 1].wait()
        proj[w] = lax.dot_general(
            feats[w], weights[w], (((0,), (0,)), ((), ())), preferred_element_type=F32
        )
        for t in range(n_tp):
            proj_send[w, t] = proj[w, t * rows:(t + 1) * rows].astype(BF16)
    pl.semaphore_wait(barrier, greeted)
    for w in (1, 0):
        for d in range(1, n_tp):
            t = lax.rem(tp + d, n_tp)
            pltpu.make_async_remote_copy(
                src_ref=proj_send.at[w, t], dst_ref=proj_recv.at[w, d - 1],
                send_sem=proj_sems.at[w, 0], recv_sem=proj_sems.at[w, 1],
                device_id=(loop, z, t), device_id_type=MESH,
            ).start()
    def send_feat(w, device):
        pltpu.make_async_remote_copy(
            src_ref=feats.at[w], dst_ref=feat_all.at[loop],
            send_sem=feat_sems.at[0], recv_sem=feat_sems.at[1],
            device_id=device, device_id_type=MESH,
        ).start()

    send_feat(1 - core, partner)
    for w in range(2):
        for h in range(1, n_hi):
            send_feat(w, (lax.rem(loop - core + w + 2 * h, n_loop), z, tp))
    feat_all[loop] = feats[core]

    def embed(w):
        wait_bytes(proj_recv.at[w, pl.ds(0, n_tp - 1)], proj_sems.at[w, 1])
        total = proj[w, pl.ds(pl.multiple_of(tp * rows, rows), rows)]
        for d in range(n_tp - 1):
            total = total + proj_recv[w, d].astype(F32)
        inverse = lax.rsqrt(jnp.sum(total * total, axis=-1, keepdims=True) + 1e-06)
        unit = total * inverse
        (img_all, txt_all)[w][0:rows] = unit.astype(BF16)
        return unit, inverse

    def slot(i):
        return pl.ds(i * rows, rows)

    def lane(right, m):
        return m if right else (n_sub - m) % n_sub

    def send_txt(k):
        ring_sends(
            n_sub, STRIDE, k,
            source=lambda right, m: txt_all.at[slot(lane(right, m))],
            target=lambda right, m: txt_all.at[slot(lane(right, m))],
            device=in_ring, send_sem=txt_send,
            recv_sem=lambda right, m: txt_gather.at[lane(right, m)],
        )

    def txt_arrived(right, m):
        wait_bytes(txt_all.at[slot(lane(right, m))], txt_gather.at[lane(right, m)])

    txt_unit, txt_inverse = embed(1)
    send_txt(0)
    img_unit, img_inverse = embed(0)
    for d in range(1, chips):
        pltpu.make_async_remote_copy(
            src_ref=img_all.at[slot(0)], dst_ref=img_all.at[slot(d)],
            send_sem=img_send, recv_sem=img_gather.at[d],
            device_id=in_plane(d, core), device_id_type=MESH,
        ).start()
    half_img = chips * rows
    group = max(1, chips // 4)

    def forward_img():
        for g in range(0, chips, group):
            for d in range(max(g, 1), g + group):
                wait_bytes(img_all.at[slot(d)], img_gather.at[d])
            pltpu.make_async_remote_copy(
                src_ref=img_all.at[g * rows:(g + group) * rows],
                dst_ref=img_all.at[half_img + g * rows:half_img + (g + group) * rows],
                send_sem=img_core.at[0], recv_sem=img_core.at[1],
                device_id=partner, device_id_type=MESH,
            ).start()

    steps = -(-reach(n_sub, True) // STRIDE)
    for k in range(1, steps):
        if k == steps - 1:
            forward_img()
        for right in (True, False):
            if STRIDE * k < reach(n_sub, right):
                txt_arrived(right, STRIDE * k)
        send_txt(k)
    if steps == 1:
        forward_img()
    for right in (True, False):
        for m in range(1, reach(n_sub, right) + 1):
            if m % STRIDE or m == reach(n_sub, right):
                txt_arrived(right, m)
    wait_bytes(img_all.at[half_img:2 * half_img], img_core.at[1])

    scale = scale_ref[0]
    bias = bias_ref[0]
    n_img, n_txt = 2 * half_img, n_sub * rows
    step = min(128, half_img)
    for i in range(0, n_img, step):
        logits = scale * lax.dot_general(
            img_all[i:i + step], txt_all[...], (((1,), (1,)), ((), ())),
            preferred_element_type=F32,
        ) + bias
        value = jax.nn.sigmoid(logits)
        if i < rows:
            r = lax.broadcasted_iota(jnp.int32, logits.shape, 0) + i
            c = lax.broadcasted_iota(jnp.int32, logits.shape, 1)
            value = value - jnp.where((r == c) & (r < rows), 1.0, 0.0)
        slope[i:i + step] = (scale * value / pairs).astype(BF16)

    def img_grad(start):
        for i in range(start, start + half_img, step):
            d_img = jnp.dot(slope[i:i + step], txt_all[...], preferred_element_type=F32)
            if i == 0:
                img_own[...] = d_img[0:rows]
            img_part[i:i + step] = d_img.astype(BF16)

    img_grad(half_img)
    pltpu.make_async_remote_copy(
        src_ref=img_part.at[half_img:n_img], dst_ref=img_pair,
        send_sem=img_pair_sems.at[0], recv_sem=img_pair_sems.at[1],
        device_id=partner, device_id_type=MESH,
    ).start()
    width_txt = min(128, n_txt)
    for i in range(0, n_txt, width_txt):
        d_txt = lax.dot_general(
            slope[:, i:i + width_txt], img_all[...], (((0,), (0,)), ((), ())),
            preferred_element_type=F32,
        )
        if i == 0:
            txt_own[...] = d_txt[0:rows]
        txt_part[i:i + width_txt] = d_txt.astype(BF16)

    def share_img():
        img_grad(0)
        wait_bytes(img_pair, img_pair_sems.at[1])
        for d in range(1, chips):
            img_part[slot(d)] = (
                img_part[slot(d)].astype(F32) + img_pair[slot(d)].astype(F32)
            ).astype(BF16)
            pltpu.make_async_remote_copy(
                src_ref=img_part.at[slot(d)], dst_ref=img_recv.at[slot(d - 1)],
                send_sem=img_sum_sems.at[0], recv_sem=img_sum_sems.at[1],
                device_id=in_plane(chips - d, core), device_id_type=MESH,
            ).start()

    spot = pl.ds(pl.multiple_of((loop * n_tp + tp) * rows, rows), rows)

    def send_back(w, unit, inverse, upstream):
        inner = jnp.sum(unit * upstream, axis=-1, keepdims=True)
        back[w] = ((upstream - unit * inner) * inverse).astype(BF16)

        def send(device):
            pltpu.make_async_remote_copy(
                src_ref=back.at[w], dst_ref=back_all.at[spot],
                send_sem=back_sems.at[0], recv_sem=back_sems.at[1],
                device_id=device, device_id_type=MESH,
            ).start()

        for d in range(1, chips):
            send(in_plane(d, w))

        @pl.when(core == w)
        def _():
            back_all[spot] = back[w]

        @pl.when(core != w)
        def _():
            send(partner)

    def finish_img():
        wait_bytes(img_recv.at[0:(chips - 1) * rows], img_sum_sems.at[1])
        d_img = img_own[...] + img_pair[slot(0)].astype(F32)
        for d in range(chips - 1):
            d_img = d_img + img_recv[slot(d)].astype(F32)
        send_back(0, img_unit, img_inverse, d_img)

    def between(at, last):
        if at == 0:
            share_img()
        if at == last:
            finish_img()

    d_txt = txt_own[...] + ring_sum(
        n_sub, STRIDE,
        part=lambda right, d: txt_part.at[slot(lane(not right, d))],
        landing=lambda right, d: txt_recv.at[slot(lane(right, d))],
        device=in_ring, send_sem=txt_sum_send,
        recv_sem=lambda right, d: txt_sum.at[lane(right, d)],
        between=between,
    )
    send_back(1, txt_unit, txt_inverse, d_txt)
    wait_bytes(feat_all.at[0:n_loop - 1], feat_sems.at[1])
    wait_bytes(back_all.at[0:(2 * chips - 1) * rows], back_sems.at[1])

    total = jnp.zeros((depth, width), F32)
    for i in range(n_loop):
        total = total + jnp.dot(
            feat_all[i], back_all[i * batch:(i + 1) * batch], preferred_element_type=F32
        )
    both[...] = total
    half = depth // 2
    tiles = width // 128
    my_half = both[pl.ds(pl.multiple_of(hi * half, half), half)]
    for k in range(tiles):
        grad[k * half:(k + 1) * half] = my_half[:, k * 128:(k + 1) * 128]
    if tiles * half < grad.shape[0]:
        grad[tiles * half:] = jnp.zeros((grad.shape[0] - tiles * half, 128), F32)
    grad_part[...] = grad[...].astype(BF16)
    chunk = grad.shape[0] // n_sub

    def piece(owner):
        return pl.ds(pl.multiple_of(lax.rem(owner + n_sub, n_sub) * chunk, chunk), chunk)

    def tile_slot(i):
        return pl.ds(i * chunk, chunk)

    far_first = sorted(range(1, n_sub), key=lambda d: (-min(d, n_sub - d), d))
    for d in far_first:
        pltpu.make_async_remote_copy(
            src_ref=grad_part.at[piece(z + d)], dst_ref=grad_recv.at[d - 1],
            send_sem=grad_sems.at[0], recv_sem=grad_sems.at[1],
            device_id=in_ring(d), device_id_type=MESH,
        ).start()
    done = grad[piece(z)]
    wait_bytes(grad_recv, grad_sems.at[1])
    for d in range(n_sub - 1):
        done = done + grad_recv[d].astype(F32)
    held = full.at[core, hi]
    other = full.at[core, 1 - hi]
    full[core, hi, 0:chunk] = done.astype(BF16)

    def held_slot(right, m):
        return held.at[tile_slot(lane(right, m))]

    def send_full(k):
        ring_sends(
            n_sub, FULL_STRIDE, k, source=held_slot, target=held_slot,
            device=in_ring, send_sem=full_send,
            recv_sem=lambda right, m: full_gather.at[lane(right, m)],
        )

    def full_arrived(right, m):
        wait_bytes(held_slot(right, m), full_gather.at[lane(right, m)])

    def to_core(ref):
        pltpu.make_async_remote_copy(
            src_ref=ref, dst_ref=ref, send_sem=core_sems.at[0], recv_sem=core_sems.at[1],
            device_id=partner, device_id_type=MESH,
        ).start()

    def pass_on(g):
        s, e = spans[g]
        ref = held.at[s * chunk:e * chunk]
        pltpu.make_async_remote_copy(
            src_ref=ref, dst_ref=ref, send_sem=hi_send, recv_sem=hi_gather.at[g],
            device_id=across, device_id_type=MESH,
        ).start()
        to_core(ref)

    near_r, near_l = (min(FULL_STRIDE, reach(n_sub, right)) for right in (True, False))
    spans = [(0, near_r + 1), (n_sub - near_l, n_sub), (near_r + 1, n_sub - near_l)]
    send_full(0)
    for right in (True, False):
        if FULL_STRIDE < reach(n_sub, right):
            full_arrived(right, FULL_STRIDE)
    send_full(1)
    for g, right in enumerate((True, False)):
        for m in range(1, min(FULL_STRIDE, reach(n_sub, right)) + 1):
            if m != FULL_STRIDE or m == reach(n_sub, right):
                full_arrived(right, m)
        if spans[g][0] < spans[g][1]:
            pass_on(g)
    for right in (True, False):
        for m in range(FULL_STRIDE + 1, reach(n_sub, right) + 1):
            full_arrived(right, m)
    if spans[2][0] < spans[2][1]:
        pass_on(2)
    for g, (s, e) in enumerate(spans):
        if s < e:
            ref = other.at[s * chunk:e * chunk]
            wait_bytes(ref, hi_gather.at[g])
            to_core(ref)
    wait_bytes(full.at[1 - core], core_sems.at[1])
    store = pltpu.make_async_copy(full, full_out, store_sem)
    store.start()
    store.wait()

    for w in range(2):
        wait_bytes(proj_send.at[w, pl.ds(0, n_tp - 1)], proj_sems.at[w, 0])
    wait_bytes(feat_all.at[0:n_loop - 1], feat_sems.at[0])
    wait_bytes(img_all.at[rows:half_img], img_send)
    wait_bytes(img_all.at[0:half_img], img_core.at[0])
    wait_bytes(txt_all.at[rows:n_txt], txt_send)
    wait_bytes(img_pair, img_pair_sems.at[0])
    wait_bytes(img_recv.at[0:(chips - 1) * rows], img_sum_sems.at[0])
    wait_bytes(txt_all.at[rows:n_txt], txt_sum_send)
    wait_bytes(back_all.at[0:(2 * chips - 1) * rows], back_sems.at[0])
    wait_bytes(grad_recv, grad_sems.at[0])
    wait_bytes(held.at[chunk:n_sub * chunk], full_send)
    wait_bytes(held, hi_send)
    wait_bytes(full.at[core], core_sems.at[0])


def lay_out(n_sub, half, tiles, full_hbm, outi_hbm, outt_hbm, full, ordered, both, load_sems, store_sems):
    z = lax.axis_index("sub")
    chunk = full.shape[2] // n_sub
    parts = [(w, h) for w in range(2) for h in range(2)]
    loads = [
        pltpu.make_async_copy(full_hbm.at[w, h], full.at[w, h], load_sems.at[w, h])
        for w, h in parts
    ]
    for load in loads:
        load.start()
    stores = []
    for (w, h), load in zip(parts, loads):
        load.wait()
        for d in range(n_sub):
            at = lax.rem(z - d + n_sub, n_sub) * chunk
            ordered[pl.ds(pl.multiple_of(at, chunk), chunk)] = (
                full[w, h, d * chunk:(d + 1) * chunk].astype(F32)
            )
        rows = slice(h * half, (h + 1) * half)
        for k in range(tiles):
            both[w, rows, k * 128:(k + 1) * 128] = ordered[k * half:(k + 1) * half]
        store = pltpu.make_async_copy(
            both.at[w, rows], (outi_hbm, outt_hbm)[w].at[rows], store_sems.at[w, h]
        )
        store.start()
        stores.append(store)
    for store in stores:
        store.wait()


def per_device(n_loop, n_sub, n_tp, img_feat, txt_feat, img_weight, txt_weight, scale, bias):
    depth, width = img_weight.shape
    batch = img_feat.shape[0]
    rows = batch // n_tp
    half_img, n_txt = n_loop // 2 * n_tp * rows, n_sub * rows
    n_img = 2 * half_img
    used = width // 128 * depth // 2
    chunk = up16(-(-used // n_sub))
    dma = pltpu.SemaphoreType.DMA
    smem = pl.BlockSpec(memory_space=pltpu.SMEM)
    hbm = pl.BlockSpec(memory_space=pltpu.HBM)
    full = pl.pallas_call(
        functools.partial(kernel, n_loop, n_sub, n_tp),
        out_shape=jax.ShapeDtypeStruct((2, 2, n_sub * chunk, 128), BF16),
        in_specs=[smem, smem] + [hbm] * 4,
        out_specs=hbm,
        scratch_shapes=[
            pltpu.VMEM((2, depth, batch), BF16),
            pltpu.VMEM((2, depth, width), BF16),
            pltpu.VMEM((2, batch, width), F32),
            pltpu.VMEM((2, n_tp, rows, width), BF16),
            pltpu.VMEM((2, n_tp - 1, rows, width), BF16),
            pltpu.VMEM((n_img, width), BF16),
            pltpu.VMEM((n_txt, width), BF16),
            pltpu.VMEM((n_img, n_txt), BF16),
            pltpu.VMEM((n_img, width), BF16),
            pltpu.VMEM((n_txt, width), BF16),
            pltpu.VMEM((half_img, width), BF16),
            pltpu.VMEM((half_img, width), BF16),
            pltpu.VMEM((n_txt, width), BF16),
            pltpu.VMEM((rows, width), F32),
            pltpu.VMEM((rows, width), F32),
            pltpu.VMEM((2, rows, width), BF16),
            pltpu.VMEM((n_img, width), BF16),
            pltpu.VMEM((n_loop, depth, batch), BF16),
            pltpu.VMEM((depth, width), F32),
            pltpu.VMEM((n_sub * chunk, 128), F32),
            pltpu.VMEM((n_sub * chunk, 128), BF16),
            pltpu.VMEM((n_sub - 1, chunk, 128), BF16),
            pltpu.VMEM((2, 2, n_sub * chunk, 128), BF16),
            dma((2, 2)),
            dma((2,)),
            dma((2, 2)),
            dma,
            dma((n_loop // 2 * n_tp,)),
            dma((2,)),
            dma,
            dma((n_sub,)),
            dma((2,)),
            dma((2,)),
            dma,
            dma((n_sub,)),
            dma((2,)),
            dma((2,)),
            dma,
            dma((n_sub,)),
            dma,
            dma((3,)),
            dma((2,)),
            dma,
        ],
        compiler_params=pltpu.CompilerParams(
            collective_id=0, has_side_effects=True, vmem_limit_bytes=60 * 1024 * 1024
        ),
        cost_estimate=pl.CostEstimate(
            flops=6 * n_img * n_txt * width, bytes_accessed=4 * depth * width * 3, transcendentals=0
        ),
    )(scale, bias, img_feat.T, txt_feat.T, img_weight, txt_weight)
    out = jax.ShapeDtypeStruct((depth, width), F32)
    return pl.pallas_call(
        functools.partial(lay_out, n_sub, depth // 2, width // 128),
        out_shape=(out, out),
        in_specs=[hbm],
        out_specs=(hbm, hbm),
        scratch_shapes=[
            pltpu.VMEM((2, 2, n_sub * chunk, 128), BF16),
            pltpu.VMEM((n_sub * chunk, 128), F32),
            pltpu.VMEM((2, depth, width), F32),
            dma((2, 2)),
            dma((2, 2)),
        ],
        compiler_params=pltpu.CompilerParams(vmem_limit_bytes=60 * 1024 * 1024),
    )(full)


def solution(mesh):
    placed = (
        P(("loop", "sub"), "tp"),
        P(("loop", "sub"), "tp"),
        P("tp", None),
        P("tp", None),
        P(),
        P(),
    )
    sizes = (mesh.shape["loop"], mesh.shape["sub"], mesh.shape["tp"])
    return jax.shard_map(
        functools.partial(per_device, *sizes),
        mesh=mesh,
        in_specs=placed,
        out_specs=(P("tp", None), P("tp", None)),
        check_vma=False,
    )
```

```python
import functools

import jax
import jax.numpy as jnp
from jax import lax
from jax.experimental import pallas as pl
from jax.experimental.pallas import tpu as pltpu
from jax.sharding import PartitionSpec as P

MESH = pl.DeviceIdType.MESH
BF16 = jnp.bfloat16
F32 = jnp.float32
STRIDE = 3
FULL_STRIDE = 4
LATE = True


def up16(n):
    return -(-n // 16) * 16


def wait_bytes(ref, sem):
    pltpu.make_async_copy(ref, ref, sem).wait()


def reach(n, right):
    return n // 2 if right else (n - 1) // 2


def ring_sends(n, stride, k, source, target, device, send_sem, recv_sem, hops):
    for j in hops:
        for right in (True, False):
            m = stride * k + j
            if m <= reach(n, right):
                pltpu.make_async_remote_copy(
                    src_ref=source(right, stride * k),
                    dst_ref=target(right, m),
                    send_sem=send_sem,
                    recv_sem=recv_sem(right, m),
                    device_id=device(j if right else -j),
                    device_id_type=MESH,
                ).start()


def ring_sum(n, stride, part, landing, device, send_sem, recv_sem, between):
    def send(right, d):
        hop = d - stride * ((d - 1) // stride)
        pltpu.make_async_remote_copy(
            src_ref=part(right, d),
            dst_ref=landing(right, d),
            send_sem=send_sem,
            recv_sem=recv_sem(right, d),
            device_id=device(hop if right else -hop),
            device_id_type=MESH,
        ).start()

    def collect(right, d, value):
        for m in range(d + 1, min(d + stride, reach(n, right)) + 1):
            ref = landing(right, m)
            wait_bytes(ref, recv_sem(right, m))
            value = value + ref[...].astype(F32)
        return value

    later, last = [], []
    for d in range(reach(n, True), 0, -1):
        for right in (True, False):
            if d > reach(n, right):
                continue
            if d % stride == 0 and d < reach(n, right):
                later.append((right, d))
            elif LATE and d < stride:
                last.append((right, d))
            else:
                send(right, d)
    steps = sorted({d for _, d in later}, reverse=True)
    for at, d in enumerate(steps + [0]):
        between(at, len(steps))
        for right in (True, False):
            if (right, d) in later:
                ref = part(right, d)
                ref[...] = collect(right, d, ref[...].astype(F32)).astype(BF16)
                send(right, d)
        if at == 0:
            for right, d in last:
                send(right, d)
    return collect(False, 0, collect(True, 0, jnp.zeros(part(True, 0).shape, F32)))


def kernel(
    n_loop, n_sub, n_tp,
    scale_ref, bias_ref, imgf_hbm, txtf_hbm, imgw_hbm, txtw_hbm,
    full_out,
    feats, weights, proj, proj_recv, img_all, txt_all, slope,
    img_part, txt_part, img_pair, img_recv, txt_recv, img_own, txt_own,
    back, back_all, feat_all,
    both, grad, half_send, half_recv, grad_part, grad_recv, full,
    load_sems, feat_sems, proj_sems, img_send, img_gather, img_core, txt_send, txt_gather,
    img_sum_sems, img_pair_sems, txt_sum_send, txt_sum, back_sems, half_sems, grad_sems,
    full_send, full_gather, hi_send, hi_gather, core_sems, store_sem,
):
    _, depth, batch = feats.shape
    width = weights.shape[2]
    rows = batch // n_tp
    n_hi = n_loop // 2
    chips = n_hi * n_tp
    pairs = batch * n_loop * n_sub
    loop = lax.axis_index("loop")
    z = lax.axis_index("sub")
    tp = lax.axis_index("tp")
    core = lax.rem(loop, 2)
    hi = loop // 2
    chip = hi * n_tp + tp
    partner = (loop + 1 - 2 * core, z, tp)
    across = (lax.rem(loop + 2, n_loop), z, tp)

    def in_plane(d, to_core):
        p = lax.rem(chip + d, chips)
        return (p // n_tp * 2 + to_core, z, lax.rem(p, n_tp))

    def in_ring(d):
        return (loop, lax.rem(z + d + n_sub, n_sub), tp)

    def greet(device):
        pl.semaphore_signal(barrier, inc=1, device_id=device, device_id_type=MESH)

    barrier = pltpu.get_barrier_semaphore()
    ring = sorted({d % n_sub for j in range(1, STRIDE + 1) for d in (j, -j)} - {0})
    for d in ring:
        greet(in_ring(d))
    for d in range(1, chips):
        greet(in_plane(d, core))
    greet(partner)
    for d in range(1, n_tp):
        greet((loop + 1 - 2 * core, z, lax.rem(tp + d, n_tp)))
    greeted = len(ring) + chips + n_tp - 1

    loads = []
    for w, (f_hbm, w_hbm) in ((1, (txtf_hbm, txtw_hbm)), (0, (imgf_hbm, imgw_hbm))):
        for i, (src, dst) in enumerate(((f_hbm, feats.at[w]), (w_hbm, weights.at[w]))):
            load = pltpu.make_async_copy(src, dst, load_sems.at[w, i])
            load.start()
            loads.append(load)
    def project(w):
        for load in loads[2 * (1 - w):2 * (2 - w)]:
            load.wait()
        proj[w] = lax.dot_general(
            feats[w], weights[w], (((0,), (0,)), ((), ())), preferred_element_type=F32
        )
    project(1)
    full[...] = jnp.zeros(full.shape, BF16)
    grad_recv[...] = jnp.zeros(grad_recv.shape, BF16)
    pl.semaphore_wait(barrier, greeted)

    def send_proj(w):
        for d in range(1, n_tp):
            t = lax.rem(tp + d, n_tp)
            pltpu.make_async_remote_copy(
                src_ref=proj.at[w, pl.ds(pl.multiple_of(t * rows, rows), rows)],
                dst_ref=proj_recv.at[w, d - 1],
                send_sem=proj_sems.at[w, 0], recv_sem=proj_sems.at[w, 1],
                device_id=(loop, z, t), device_id_type=MESH,
            ).start()
    send_proj(1)
    project(0)

    def embed(w):
        wait_bytes(proj_recv.at[w, pl.ds(0, n_tp - 1)], proj_sems.at[w, 1])
        total = proj[w, pl.ds(pl.multiple_of(tp * rows, rows), rows)]
        for d in range(n_tp - 1):
            total = total + proj_recv[w, d]
        inverse = lax.rsqrt(jnp.sum(total * total, axis=-1, keepdims=True) + 1e-06)
        unit = total * inverse
        (img_all, txt_all)[w][0:rows] = unit.astype(BF16)
        return unit, inverse

    def slot(i):
        return pl.ds(i * rows, rows)

    def lane(right, m):
        return m if right else (n_sub - m) % n_sub

    def send_txt(k, hops):
        ring_sends(
            n_sub, STRIDE, k,
            source=lambda right, m: txt_all.at[slot(lane(right, m))],
            target=lambda right, m: txt_all.at[slot(lane(right, m))],
            device=in_ring, send_sem=txt_send,
            recv_sem=lambda right, m: txt_gather.at[lane(right, m)], hops=hops,
        )

    def txt_arrived(right, m):
        wait_bytes(txt_all.at[slot(lane(right, m))], txt_gather.at[lane(right, m)])

    txt_unit, txt_inverse = embed(1)
    send_txt(0, [STRIDE])
    send_proj(0)
    pltpu.make_async_remote_copy(
        src_ref=feats.at[1 - core], dst_ref=feat_all.at[core],
        send_sem=feat_sems.at[0], recv_sem=feat_sems.at[1],
        device_id=partner, device_id_type=MESH,
    ).start()
    feat_all[core] = feats[core]
    if not LATE:
        send_txt(0, range(STRIDE - 1, 0, -1))
    if LATE:
        send_txt(0, range(STRIDE - 1, 0, -1))
    half_img = chips * rows
    group = max(1, chips // 4)

    def forward_img():
        for g in range(0, chips, group):
            for d in range(max(g, 1), g + group):
                wait_bytes(img_all.at[slot(d)], img_gather.at[d])
            pltpu.make_async_remote_copy(
                src_ref=img_all.at[g * rows:(g + group) * rows],
                dst_ref=img_all.at[half_img + g * rows:half_img + (g + group) * rows],
                send_sem=img_core.at[0], recv_sem=img_core.at[1],
                device_id=partner, device_id_type=MESH,
            ).start()

    steps = -(-reach(n_sub, True) // STRIDE)
    for k in range(1, min(2, steps)):
        for right in (True, False):
            if STRIDE * k < reach(n_sub, right):
                txt_arrived(right, STRIDE * k)
        send_txt(k, range(STRIDE, 0, -1))
    img_unit, img_inverse = embed(0)
    for d in range(1, chips):
        pltpu.make_async_remote_copy(
            src_ref=img_all.at[slot(0)], dst_ref=img_all.at[slot(d)],
            send_sem=img_send, recv_sem=img_gather.at[d],
            device_id=in_plane(d, core), device_id_type=MESH,
        ).start()
    for k in range(2, steps):
        for right in (True, False):
            if STRIDE * k < reach(n_sub, right):
                txt_arrived(right, STRIDE * k)
        send_txt(k, range(STRIDE, 0, -1))
    forward_img()
    for right in (True, False):
        for m in range(1, reach(n_sub, right) + 1):
            if m % STRIDE or m == reach(n_sub, right):
                txt_arrived(right, m)
    wait_bytes(img_all.at[half_img:2 * half_img], img_core.at[1])

    scale = scale_ref[0]
    bias = bias_ref[0]
    n_img, n_txt = 2 * half_img, n_sub * rows
    step = min(128, half_img)
    for i in range(0, n_img, step):
        logits = scale * lax.dot_general(
            img_all[i:i + step], txt_all[...], (((1,), (1,)), ((), ())),
            preferred_element_type=F32,
        ) + bias
        value = jax.nn.sigmoid(logits)
        if i < rows:
            r = lax.broadcasted_iota(jnp.int32, logits.shape, 0) + i
            c = lax.broadcasted_iota(jnp.int32, logits.shape, 1)
            value = value - jnp.where((r == c) & (r < rows), 1.0, 0.0)
        slope[i:i + step] = (scale * value / pairs).astype(BF16)

    def img_grad(start):
        for i in range(start, start + half_img, step):
            d_img = jnp.dot(slope[i:i + step], txt_all[...], preferred_element_type=F32)
            if i == 0:
                img_own[...] = d_img[0:rows]
            img_part[i:i + step] = d_img.astype(BF16)

    img_grad(half_img)
    pltpu.make_async_remote_copy(
        src_ref=img_part.at[half_img:n_img], dst_ref=img_pair,
        send_sem=img_pair_sems.at[0], recv_sem=img_pair_sems.at[1],
        device_id=partner, device_id_type=MESH,
    ).start()
    width_txt = min(128, n_txt)
    for i in range(0, n_txt, width_txt):
        d_txt = lax.dot_general(
            slope[:, i:i + width_txt], img_all[...], (((0,), (0,)), ((), ())),
            preferred_element_type=F32,
        )
        if i == 0:
            txt_own[...] = d_txt[0:rows]
        txt_part[i:i + width_txt] = d_txt.astype(BF16)

    def share_img():
        img_grad(0)
        wait_bytes(img_pair, img_pair_sems.at[1])
        for d in range(1, chips):
            img_part[slot(d)] = (
                img_part[slot(d)].astype(F32) + img_pair[slot(d)].astype(F32)
            ).astype(BF16)
            pltpu.make_async_remote_copy(
                src_ref=img_part.at[slot(d)], dst_ref=img_recv.at[slot(d - 1)],
                send_sem=img_sum_sems.at[0], recv_sem=img_sum_sems.at[1],
                device_id=in_plane(chips - d, core), device_id_type=MESH,
            ).start()

    spot = pl.ds(pl.multiple_of((core * n_tp + tp) * rows, rows), rows)

    def send_back(w, unit, inverse, upstream):
        inner = jnp.sum(unit * upstream, axis=-1, keepdims=True)
        back[w] = ((upstream - unit * inner) * inverse).astype(BF16)

        def send(device):
            pltpu.make_async_remote_copy(
                src_ref=back.at[w], dst_ref=back_all.at[spot],
                send_sem=back_sems.at[0], recv_sem=back_sems.at[1],
                device_id=device, device_id_type=MESH,
            ).start()

        for d in range(1, n_tp):
            send((loop - core + w, z, lax.rem(tp + d, n_tp)))

        @pl.when(core == w)
        def _():
            back_all[spot] = back[w]

        @pl.when(core != w)
        def _():
            send(partner)

    def finish_img():
        wait_bytes(img_recv.at[0:(chips - 1) * rows], img_sum_sems.at[1])
        d_img = img_own[...] + img_pair[slot(0)].astype(F32)
        for d in range(chips - 1):
            d_img = d_img + img_recv[slot(d)].astype(F32)
        send_back(0, img_unit, img_inverse, d_img)

    def between(at, last):
        if at == 0:
            share_img()
        if at == last:
            finish_img()

    d_txt = txt_own[...] + ring_sum(
        n_sub, STRIDE,
        part=lambda right, d: txt_part.at[slot(lane(not right, d))],
        landing=lambda right, d: txt_recv.at[slot(lane(right, d))],
        device=in_ring, send_sem=txt_sum_send,
        recv_sem=lambda right, d: txt_sum.at[lane(right, d)],
        between=between,
    )
    send_back(1, txt_unit, txt_inverse, d_txt)
    wait_bytes(feat_all.at[0], feat_sems.at[1])
    wait_bytes(back_all.at[0:(2 * n_tp - 1) * rows], back_sems.at[1])

    total = jnp.zeros((depth, width), F32)
    for i in range(2):
        total = total + jnp.dot(
            feat_all[i], back_all[i * batch:(i + 1) * batch], preferred_element_type=F32
        )
    both[...] = total
    half = depth // 2
    tiles = width // 128
    used = tiles * half

    def unfold(h):
        picked = both[pl.ds(pl.multiple_of(h * half, half), half)]
        for k in range(tiles):
            grad[k * half:(k + 1) * half] = picked[:, k * 128:(k + 1) * 128]

    if used < grad.shape[0]:
        grad[used:] = jnp.zeros((grad.shape[0] - used, 128), F32)
    unfold(1 - hi)
    sent = half_send.shape[0]
    half_send[...] = grad[0:sent].astype(BF16)
    chunk = grad.shape[0] // n_sub
    owners = -(-used // chunk)
    parts = [(0, owners)]
    for i, (lo, up) in enumerate(parts):
        span = slice(lo * chunk, min(up * chunk, sent))
        pltpu.make_async_remote_copy(
            src_ref=half_send.at[span], dst_ref=half_recv.at[span],
            send_sem=half_sems.at[i, 0], recv_sem=half_sems.at[i, 1],
            device_id=across, device_id_type=MESH,
        ).start()
    unfold(hi)

    def piece(owner):
        return pl.ds(pl.multiple_of(lax.rem(owner + n_sub, n_sub) * chunk, chunk), chunk)

    def tile_slot(i):
        return pl.ds(i * chunk, chunk)

    def is_owner(device):
        return lax.rem(device + n_sub, n_sub) < owners

    far_first = sorted(range(1, n_sub), key=lambda d: (-min(d, n_sub - d), d))

    def send_chunk(d):
        @pl.when(is_owner(z + d))
        def _():
            pltpu.make_async_remote_copy(
                src_ref=grad_part.at[piece(z + d)], dst_ref=grad_recv.at[d - 1],
                send_sem=grad_sems.at[0], recv_sem=grad_sems.at[1],
                device_id=in_ring(d), device_id_type=MESH,
            ).start()

    for i, (lo, up) in enumerate(parts):
        span = slice(lo * chunk, min(up * chunk, sent))
        wait_bytes(half_recv.at[span], half_sems.at[i, 1])
        grad[span] = grad[span] + half_recv[span].astype(F32)
        grad_part[lo * chunk:up * chunk] = grad[lo * chunk:up * chunk].astype(BF16)
    for d in far_first:
        send_chunk(d)

    @pl.when(is_owner(z))
    def _():
        wait_bytes(grad_recv, grad_sems.at[1])
    done = grad[piece(z)]
    for d in range(n_sub - 1):
        done = done + grad_recv[d].astype(F32)
    held = full.at[core, hi]
    other = full.at[core, 1 - hi]
    full[core, hi, 0:chunk] = done.astype(BF16)

    def held_slot(right, m):
        return held.at[tile_slot(lane(right, m))]

    def origin(right, m):
        return is_owner(z - m if right else z + m)

    def full_targets(k, right):
        first = FULL_STRIDE * k + 1
        return range(first, min(first + FULL_STRIDE - 1, reach(n_sub, right)) + 1)

    def send_full(k, right):
        for m in reversed(full_targets(k, right)):
            hop = m - FULL_STRIDE * k
            pltpu.make_async_remote_copy(
                src_ref=held_slot(right, FULL_STRIDE * k), dst_ref=held_slot(right, m),
                send_sem=full_send, recv_sem=full_gather.at[lane(right, m)],
                device_id=in_ring(hop if right else -hop), device_id_type=MESH,
            ).start()

    def full_sent(k, right):
        for m in full_targets(k, right):
            wait_bytes(held_slot(right, 0), full_send)

    def full_arrived(right, m):
        @pl.when(origin(right, m))
        def _():
            wait_bytes(held_slot(right, m), full_gather.at[lane(right, m)])

    def by_origin(action):
        for k in range(2):
            for right in (True, False):
                if len(full_targets(k, right)):
                    pl.when(origin(right, FULL_STRIDE * k))(functools.partial(action, k, right))

    def to_core(ref):
        pltpu.make_async_remote_copy(
            src_ref=ref, dst_ref=ref, send_sem=core_sems.at[0], recv_sem=core_sems.at[1],
            device_id=partner, device_id_type=MESH,
        ).start()

    def pass_on(g):
        s, e = spans[g]
        ref = held.at[s * chunk:e * chunk]
        pltpu.make_async_remote_copy(
            src_ref=ref, dst_ref=ref, send_sem=hi_send, recv_sem=hi_gather.at[g],
            device_id=across, device_id_type=MESH,
        ).start()
        to_core(ref)

    near_r, near_l = (min(FULL_STRIDE, reach(n_sub, right)) for right in (True, False))
    spans = [(0, near_r + 1), (n_sub - near_l, n_sub), (near_r + 1, n_sub - near_l)]

    def pass_full(k, right):
        if k:
            wait_bytes(
                held_slot(right, FULL_STRIDE), full_gather.at[lane(right, FULL_STRIDE)]
            )
        send_full(k, right)

    by_origin(pass_full)
    for g, right in enumerate((True, False)):
        for m in range(1, min(FULL_STRIDE, reach(n_sub, right)) + 1):
            if m != FULL_STRIDE or m == reach(n_sub, right):
                full_arrived(right, m)
        if spans[g][0] < spans[g][1]:
            pass_on(g)
    for right in (True, False):
        for m in range(FULL_STRIDE + 1, reach(n_sub, right) + 1):
            full_arrived(right, m)
    if spans[2][0] < spans[2][1]:
        pass_on(2)
    for g, (s, e) in enumerate(spans):
        if s < e:
            ref = other.at[s * chunk:e * chunk]
            wait_bytes(ref, hi_gather.at[g])
            to_core(ref)
    wait_bytes(full.at[1 - core], core_sems.at[1])
    store = pltpu.make_async_copy(full, full_out, store_sem)
    store.start()
    store.wait()

    for w in range(2):
        wait_bytes(proj_recv.at[w], proj_sems.at[w, 0])
    wait_bytes(feat_all.at[0], feat_sems.at[0])
    wait_bytes(img_all.at[rows:half_img], img_send)
    wait_bytes(img_all.at[0:half_img], img_core.at[0])
    wait_bytes(txt_all.at[rows:n_txt], txt_send)
    wait_bytes(img_pair, img_pair_sems.at[0])
    wait_bytes(img_recv.at[0:(chips - 1) * rows], img_sum_sems.at[0])
    wait_bytes(txt_all.at[rows:n_txt], txt_sum_send)
    wait_bytes(back_all.at[0:(2 * n_tp - 1) * rows], back_sems.at[0])
    for i, (lo, up) in enumerate(parts):
        wait_bytes(half_send.at[lo * chunk:min(up * chunk, sent)], half_sems.at[i, 0])
    for d in range(1, n_sub):
        @pl.when(is_owner(z + d))
        def _():
            wait_bytes(grad_recv.at[0], grad_sems.at[0])
    by_origin(full_sent)
    wait_bytes(held, hi_send)
    wait_bytes(full.at[core], core_sems.at[0])


def lay_out(n_sub, half, tiles, full_hbm, outi_hbm, outt_hbm, full, ordered, both, load_sems, store_sems):
    z = lax.axis_index("sub")
    chunk = full.shape[2] // n_sub
    parts = [(w, h) for w in range(2) for h in range(2)]
    loads = [
        pltpu.make_async_copy(full_hbm.at[w, h], full.at[w, h], load_sems.at[w, h])
        for w, h in parts
    ]
    for load in loads:
        load.start()
    stores = []
    for (w, h), load in zip(parts, loads):
        load.wait()
        for d in range(n_sub):
            at = lax.rem(z - d + n_sub, n_sub) * chunk
            ordered[pl.ds(pl.multiple_of(at, chunk), chunk)] = (
                full[w, h, d * chunk:(d + 1) * chunk].astype(F32)
            )
        rows = slice(h * half, (h + 1) * half)
        for k in range(tiles):
            both[w, rows, k * 128:(k + 1) * 128] = ordered[k * half:(k + 1) * half]
        store = pltpu.make_async_copy(
            both.at[w, rows], (outi_hbm, outt_hbm)[w].at[rows], store_sems.at[w, h]
        )
        store.start()
        stores.append(store)
    for store in stores:
        store.wait()


def per_device(n_loop, n_sub, n_tp, img_feat, txt_feat, img_weight, txt_weight, scale, bias):
    depth, width = img_weight.shape
    batch = img_feat.shape[0]
    rows = batch // n_tp
    half_img, n_txt = n_loop // 2 * n_tp * rows, n_sub * rows
    n_img = 2 * half_img
    used = width // 128 * depth // 2
    chunk = up16(-(-used // n_sub))
    dma = pltpu.SemaphoreType.DMA
    smem = pl.BlockSpec(memory_space=pltpu.SMEM)
    hbm = pl.BlockSpec(memory_space=pltpu.HBM)
    full = pl.pallas_call(
        functools.partial(kernel, n_loop, n_sub, n_tp),
        out_shape=jax.ShapeDtypeStruct((2, 2, n_sub * chunk, 128), BF16),
        in_specs=[smem, smem] + [hbm] * 4,
        out_specs=hbm,
        scratch_shapes=[
            pltpu.VMEM((2, depth, batch), BF16),
            pltpu.VMEM((2, depth, width), BF16),
            pltpu.VMEM((2, batch, width), F32),
            pltpu.VMEM((2, n_tp - 1, rows, width), F32),
            pltpu.VMEM((n_img, width), BF16),
            pltpu.VMEM((n_txt, width), BF16),
            pltpu.VMEM((n_img, n_txt), BF16),
            pltpu.VMEM((n_img, width), BF16),
            pltpu.VMEM((n_txt, width), BF16),
            pltpu.VMEM((half_img, width), BF16),
            pltpu.VMEM((half_img, width), BF16),
            pltpu.VMEM((n_txt, width), BF16),
            pltpu.VMEM((rows, width), F32),
            pltpu.VMEM((rows, width), F32),
            pltpu.VMEM((2, rows, width), BF16),
            pltpu.VMEM((2 * batch, width), BF16),
            pltpu.VMEM((2, depth, batch), BF16),
            pltpu.VMEM((depth, width), F32),
            pltpu.VMEM((n_sub * chunk, 128), F32),
            pltpu.VMEM((up16(used), 128), BF16),
            pltpu.VMEM((up16(used), 128), BF16),
            pltpu.VMEM((n_sub * chunk, 128), BF16),
            pltpu.VMEM((n_sub - 1, chunk, 128), BF16),
            pltpu.VMEM((2, 2, n_sub * chunk, 128), BF16),
            dma((2, 2)),
            dma((2,)),
            dma((2, 2)),
            dma,
            dma((n_loop // 2 * n_tp,)),
            dma((2,)),
            dma,
            dma((n_sub,)),
            dma((2,)),
            dma((2,)),
            dma,
            dma((n_sub,)),
            dma((2,)),
            dma((2, 2)),
            dma((2,)),
            dma,
            dma((n_sub,)),
            dma,
            dma((3,)),
            dma((2,)),
            dma,
        ],
        compiler_params=pltpu.CompilerParams(
            collective_id=0, has_side_effects=True, vmem_limit_bytes=60 * 1024 * 1024
        ),
        cost_estimate=pl.CostEstimate(
            flops=6 * n_img * n_txt * width, bytes_accessed=4 * depth * width * 3, transcendentals=0
        ),
    )(scale, bias, img_feat.T, txt_feat.T, img_weight, txt_weight)
    out = jax.ShapeDtypeStruct((depth, width), F32)
    return pl.pallas_call(
        functools.partial(lay_out, n_sub, depth // 2, width // 128),
        out_shape=(out, out),
        in_specs=[hbm],
        out_specs=(hbm, hbm),
        scratch_shapes=[
            pltpu.VMEM((2, 2, n_sub * chunk, 128), BF16),
            pltpu.VMEM((n_sub * chunk, 128), F32),
            pltpu.VMEM((2, depth, width), F32),
            dma((2, 2)),
            dma((2, 2)),
        ],
        compiler_params=pltpu.CompilerParams(vmem_limit_bytes=60 * 1024 * 1024),
    )(full)


def solution(mesh):
    placed = (
        P(("loop", "sub"), "tp"),
        P(("loop", "sub"), "tp"),
        P("tp", None),
        P("tp", None),
        P(),
        P(),
    )
    sizes = (mesh.shape["loop"], mesh.shape["sub"], mesh.shape["tp"])
    return jax.shard_map(
        functools.partial(per_device, *sizes),
        mesh=mesh,
        in_specs=placed,
        out_specs=(P("tp", None), P("tp", None)),
        check_vma=False,
    )
```

```python
import functools

import jax
import jax.numpy as jnp
from jax import lax
from jax.experimental import pallas as pl
from jax.experimental.pallas import tpu as pltpu
from jax.sharding import PartitionSpec as P

MESH = pl.DeviceIdType.MESH
BF16 = jnp.bfloat16
F32 = jnp.float32
STRIDE = 3
FULL_STRIDE = 4
LATE = True


def up16(n):
    return -(-n // 16) * 16


def wait_bytes(ref, sem):
    pltpu.make_async_copy(ref, ref, sem).wait()


def reach(n, right):
    return n // 2 if right else (n - 1) // 2


def ring_sends(n, stride, k, source, target, device, send_sem, recv_sem, hops):
    for j in hops:
        for right in (True, False):
            m = stride * k + j
            if m <= reach(n, right):
                pltpu.make_async_remote_copy(
                    src_ref=source(right, stride * k),
                    dst_ref=target(right, m),
                    send_sem=send_sem,
                    recv_sem=recv_sem(right, m),
                    device_id=device(j if right else -j),
                    device_id_type=MESH,
                ).start()


def ring_sum(n, stride, part, landing, device, send_sem, recv_sem, between):
    def send(right, d):
        hop = d - stride * ((d - 1) // stride)
        pltpu.make_async_remote_copy(
            src_ref=part(right, d),
            dst_ref=landing(right, d),
            send_sem=send_sem,
            recv_sem=recv_sem(right, d),
            device_id=device(hop if right else -hop),
            device_id_type=MESH,
        ).start()

    def collect(right, d, value):
        for m in range(d + 1, min(d + stride, reach(n, right)) + 1):
            ref = landing(right, m)
            wait_bytes(ref, recv_sem(right, m))
            value = value + ref[...].astype(F32)
        return value

    later, last = [], []
    for d in range(reach(n, True), 0, -1):
        for right in (True, False):
            if d > reach(n, right):
                continue
            if d % stride == 0 and d < reach(n, right):
                later.append((right, d))
            elif LATE and d < stride:
                last.append((right, d))
            else:
                send(right, d)
    steps = sorted({d for _, d in later}, reverse=True)
    for at, d in enumerate(steps + [0]):
        between(at, len(steps))
        for right in (True, False):
            if (right, d) in later:
                ref = part(right, d)
                ref[...] = collect(right, d, ref[...].astype(F32)).astype(BF16)
                send(right, d)
        if at == 0:
            for right, d in last:
                send(right, d)
    return collect(False, 0, collect(True, 0, jnp.zeros(part(True, 0).shape, F32)))


def kernel(
    n_loop, n_sub, n_tp,
    scale_ref, bias_ref, imgf_hbm, txtf_hbm, imgw_hbm, txtw_hbm,
    full_out,
    feats, weights, proj, proj_recv, img_all, txt_all, slope,
    img_part, txt_part, img_pair, img_recv, txt_recv, img_own, txt_own,
    back, back_all, feat_all,
    both, grad, half_send, half_recv, grad_part, grad_recv, full,
    load_sems, feat_sems, proj_sems, img_send, img_gather, img_core, txt_send, txt_gather,
    img_sum_sems, img_pair_sems, txt_sum_send, txt_sum, back_sems, half_sems, grad_sems,
    full_send, full_gather, hi_send, hi_gather, core_sems, store_sem,
):
    _, depth, batch = feats.shape
    width = weights.shape[2]
    rows = batch // n_tp
    n_hi = n_loop // 2
    chips = n_hi * n_tp
    pairs = batch * n_loop * n_sub
    loop = lax.axis_index("loop")
    z = lax.axis_index("sub")
    tp = lax.axis_index("tp")
    core = lax.rem(loop, 2)
    hi = loop // 2
    chip = hi * n_tp + tp
    partner = (loop + 1 - 2 * core, z, tp)
    across = (lax.rem(loop + 2, n_loop), z, tp)

    def in_plane(d, to_core):
        p = lax.rem(chip + d, chips)
        return (p // n_tp * 2 + to_core, z, lax.rem(p, n_tp))

    def in_ring(d):
        return (loop, lax.rem(z + d + n_sub, n_sub), tp)

    def greet(device):
        pl.semaphore_signal(barrier, inc=1, device_id=device, device_id_type=MESH)

    barrier = pltpu.get_barrier_semaphore()
    ring = sorted({d % n_sub for j in range(1, STRIDE + 1) for d in (j, -j)} - {0})
    for d in ring:
        greet(in_ring(d))
    for d in range(1, chips):
        greet(in_plane(d, core))
    greet(partner)
    for d in range(1, n_tp):
        greet((loop + 1 - 2 * core, z, lax.rem(tp + d, n_tp)))
    greeted = len(ring) + chips + n_tp - 1

    loads = []
    for w, (f_hbm, w_hbm) in ((1, (txtf_hbm, txtw_hbm)), (0, (imgf_hbm, imgw_hbm))):
        for i, (src, dst) in enumerate(((f_hbm, feats.at[w]), (w_hbm, weights.at[w]))):
            load = pltpu.make_async_copy(src, dst, load_sems.at[w, i])
            load.start()
            loads.append(load)
    def project(w):
        for load in loads[2 * (1 - w):2 * (2 - w)]:
            load.wait()
        proj[w] = lax.dot_general(
            feats[w], weights[w], (((0,), (0,)), ((), ())), preferred_element_type=F32
        )
    project(1)
    full[...] = jnp.zeros(full.shape, BF16)
    grad_recv[...] = jnp.zeros(grad_recv.shape, BF16)
    pl.semaphore_wait(barrier, greeted)

    def send_proj(w):
        for d in sorted(range(1, n_tp), key=lambda d: abs(2 * d - n_tp)):
            t = lax.rem(tp + d, n_tp)
            pltpu.make_async_remote_copy(
                src_ref=proj.at[w, pl.ds(pl.multiple_of(t * rows, rows), rows)],
                dst_ref=proj_recv.at[w, d - 1],
                send_sem=proj_sems.at[w, 0], recv_sem=proj_sems.at[w, 1],
                device_id=(loop, z, t), device_id_type=MESH,
            ).start()
    send_proj(1)
    project(0)
    send_proj(0)

    def embed(w):
        wait_bytes(proj_recv.at[w, pl.ds(0, n_tp - 1)], proj_sems.at[w, 1])
        total = proj[w, pl.ds(pl.multiple_of(tp * rows, rows), rows)]
        for d in range(n_tp - 1):
            total = total + proj_recv[w, d]
        inverse = lax.rsqrt(jnp.sum(total * total, axis=-1, keepdims=True) + 1e-06)
        unit = total * inverse
        (img_all, txt_all)[w][0:rows] = unit.astype(BF16)
        return unit, inverse

    def slot(i):
        return pl.ds(i * rows, rows)

    def lane(right, m):
        return m if right else (n_sub - m) % n_sub

    def send_txt(k, hops):
        ring_sends(
            n_sub, STRIDE, k,
            source=lambda right, m: txt_all.at[slot(lane(right, m))],
            target=lambda right, m: txt_all.at[slot(lane(right, m))],
            device=in_ring, send_sem=txt_send,
            recv_sem=lambda right, m: txt_gather.at[lane(right, m)], hops=hops,
        )

    def txt_arrived(right, m):
        wait_bytes(txt_all.at[slot(lane(right, m))], txt_gather.at[lane(right, m)])

    txt_unit, txt_inverse = embed(1)
    send_txt(0, [STRIDE])
    pltpu.make_async_remote_copy(
        src_ref=feats.at[1 - core], dst_ref=feat_all.at[core],
        send_sem=feat_sems.at[0], recv_sem=feat_sems.at[1],
        device_id=partner, device_id_type=MESH,
    ).start()
    feat_all[core] = feats[core]
    if not LATE:
        send_txt(0, range(STRIDE - 1, 0, -1))
    if LATE:
        send_txt(0, range(STRIDE - 1, 0, -1))
    half_img = chips * rows
    group = max(1, chips // 4)

    def forward_img():
        for g in range(0, chips, group):
            for d in range(max(g, 1), g + group):
                wait_bytes(img_all.at[slot(d)], img_gather.at[d])
            pltpu.make_async_remote_copy(
                src_ref=img_all.at[g * rows:(g + group) * rows],
                dst_ref=img_all.at[half_img + g * rows:half_img + (g + group) * rows],
                send_sem=img_core.at[0], recv_sem=img_core.at[1],
                device_id=partner, device_id_type=MESH,
            ).start()

    steps = -(-reach(n_sub, True) // STRIDE)
    for k in range(1, min(2, steps)):
        for right in (True, False):
            if STRIDE * k < reach(n_sub, right):
                txt_arrived(right, STRIDE * k)
        send_txt(k, range(STRIDE, 0, -1))
    img_unit, img_inverse = embed(0)
    for d in range(1, chips):
        pltpu.make_async_remote_copy(
            src_ref=img_all.at[slot(0)], dst_ref=img_all.at[slot(d)],
            send_sem=img_send, recv_sem=img_gather.at[d],
            device_id=in_plane(d, core), device_id_type=MESH,
        ).start()
    for k in range(2, steps):
        for right in (True, False):
            if STRIDE * k < reach(n_sub, right):
                txt_arrived(right, STRIDE * k)
        send_txt(k, range(STRIDE, 0, -1))
    forward_img()
    for right in (True, False):
        for m in range(1, reach(n_sub, right) + 1):
            if m % STRIDE or m == reach(n_sub, right):
                txt_arrived(right, m)
    wait_bytes(img_all.at[half_img:2 * half_img], img_core.at[1])

    scale = scale_ref[0]
    bias = bias_ref[0]
    n_img, n_txt = 2 * half_img, n_sub * rows
    step = min(128, half_img)
    for i in range(0, n_img, step):
        logits = scale * lax.dot_general(
            img_all[i:i + step], txt_all[...], (((1,), (1,)), ((), ())),
            preferred_element_type=F32,
        ) + bias
        value = jax.nn.sigmoid(logits)
        if i < rows:
            r = lax.broadcasted_iota(jnp.int32, logits.shape, 0) + i
            c = lax.broadcasted_iota(jnp.int32, logits.shape, 1)
            value = value - jnp.where((r == c) & (r < rows), 1.0, 0.0)
        slope[i:i + step] = (scale * value / pairs).astype(BF16)

    def img_grad(start):
        for i in range(start, start + half_img, step):
            d_img = jnp.dot(slope[i:i + step], txt_all[...], preferred_element_type=F32)
            if i == 0:
                img_own[...] = d_img[0:rows]
            img_part[i:i + step] = d_img.astype(BF16)

    img_grad(half_img)
    pltpu.make_async_remote_copy(
        src_ref=img_part.at[half_img:n_img], dst_ref=img_pair,
        send_sem=img_pair_sems.at[0], recv_sem=img_pair_sems.at[1],
        device_id=partner, device_id_type=MESH,
    ).start()
    width_txt = min(128, n_txt)
    for i in range(0, n_txt, width_txt):
        d_txt = lax.dot_general(
            slope[:, i:i + width_txt], img_all[...], (((0,), (0,)), ((), ())),
            preferred_element_type=F32,
        )
        if i == 0:
            txt_own[...] = d_txt[0:rows]
        txt_part[i:i + width_txt] = d_txt.astype(BF16)

    def share_img():
        img_grad(0)
        wait_bytes(img_pair, img_pair_sems.at[1])
        for d in range(1, chips):
            img_part[slot(d)] = (
                img_part[slot(d)].astype(F32) + img_pair[slot(d)].astype(F32)
            ).astype(BF16)
            pltpu.make_async_remote_copy(
                src_ref=img_part.at[slot(d)], dst_ref=img_recv.at[slot(d - 1)],
                send_sem=img_sum_sems.at[0], recv_sem=img_sum_sems.at[1],
                device_id=in_plane(chips - d, core), device_id_type=MESH,
            ).start()

    spot = pl.ds(pl.multiple_of((core * n_tp + tp) * rows, rows), rows)

    def send_back(w, unit, inverse, upstream):
        inner = jnp.sum(unit * upstream, axis=-1, keepdims=True)
        back[w] = ((upstream - unit * inner) * inverse).astype(BF16)

        def send(device):
            pltpu.make_async_remote_copy(
                src_ref=back.at[w], dst_ref=back_all.at[spot],
                send_sem=back_sems.at[0], recv_sem=back_sems.at[1],
                device_id=device, device_id_type=MESH,
            ).start()

        for d in range(1, n_tp):
            send((loop - core + w, z, lax.rem(tp + d, n_tp)))

        @pl.when(core == w)
        def _():
            back_all[spot] = back[w]

        @pl.when(core != w)
        def _():
            send(partner)

    def finish_img():
        wait_bytes(img_recv.at[0:(chips - 1) * rows], img_sum_sems.at[1])
        d_img = img_own[...] + img_pair[slot(0)].astype(F32)
        for d in range(chips - 1):
            d_img = d_img + img_recv[slot(d)].astype(F32)
        send_back(0, img_unit, img_inverse, d_img)

    def between(at, last):
        if at == 0:
            share_img()
        if at == last:
            finish_img()

    d_txt = txt_own[...] + ring_sum(
        n_sub, STRIDE,
        part=lambda right, d: txt_part.at[slot(lane(not right, d))],
        landing=lambda right, d: txt_recv.at[slot(lane(right, d))],
        device=in_ring, send_sem=txt_sum_send,
        recv_sem=lambda right, d: txt_sum.at[lane(right, d)],
        between=between,
    )
    send_back(1, txt_unit, txt_inverse, d_txt)
    wait_bytes(feat_all.at[0], feat_sems.at[1])
    wait_bytes(back_all.at[0:(2 * n_tp - 1) * rows], back_sems.at[1])

    total = jnp.zeros((depth, width), F32)
    for i in range(2):
        total = total + jnp.dot(
            feat_all[i], back_all[i * batch:(i + 1) * batch], preferred_element_type=F32
        )
    both[...] = total
    half = depth // 2
    tiles = width // 128
    used = tiles * half

    def unfold(h):
        picked = both[pl.ds(pl.multiple_of(h * half, half), half)]
        for k in range(tiles):
            grad[k * half:(k + 1) * half] = picked[:, k * 128:(k + 1) * 128]

    if used < grad.shape[0]:
        grad[used:] = jnp.zeros((grad.shape[0] - used, 128), F32)
    unfold(1 - hi)
    sent = half_send.shape[0]
    half_send[...] = grad[0:sent].astype(BF16)
    chunk = grad.shape[0] // n_sub
    owners = -(-used // chunk)
    parts = [(0, owners)]
    for i, (lo, up) in enumerate(parts):
        span = slice(lo * chunk, min(up * chunk, sent))
        pltpu.make_async_remote_copy(
            src_ref=half_send.at[span], dst_ref=half_recv.at[span],
            send_sem=half_sems.at[i, 0], recv_sem=half_sems.at[i, 1],
            device_id=across, device_id_type=MESH,
        ).start()
    unfold(hi)

    def piece(owner):
        return pl.ds(pl.multiple_of(lax.rem(owner + n_sub, n_sub) * chunk, chunk), chunk)

    def tile_slot(i):
        return pl.ds(i * chunk, chunk)

    def is_owner(device):
        return lax.rem(device + n_sub, n_sub) < owners

    far_first = sorted(range(1, n_sub), key=lambda d: (-min(d, n_sub - d), d))

    def send_chunk(d):
        @pl.when(is_owner(z + d))
        def _():
            pltpu.make_async_remote_copy(
                src_ref=grad_part.at[piece(z + d)], dst_ref=grad_recv.at[d - 1],
                send_sem=grad_sems.at[0], recv_sem=grad_sems.at[1],
                device_id=in_ring(d), device_id_type=MESH,
            ).start()

    for i, (lo, up) in enumerate(parts):
        span = slice(lo * chunk, min(up * chunk, sent))
        wait_bytes(half_recv.at[span], half_sems.at[i, 1])
        grad[span] = grad[span] + half_recv[span].astype(F32)
        grad_part[lo * chunk:up * chunk] = grad[lo * chunk:up * chunk].astype(BF16)
    for d in far_first:
        send_chunk(d)

    @pl.when(is_owner(z))
    def _():
        wait_bytes(grad_recv, grad_sems.at[1])
    done = grad[piece(z)]
    for d in range(n_sub - 1):
        done = done + grad_recv[d].astype(F32)
    held = full.at[core, hi]
    other = full.at[core, 1 - hi]
    full[core, hi, 0:chunk] = done.astype(BF16)

    def held_slot(right, m):
        return held.at[tile_slot(lane(right, m))]

    def origin(right, m):
        return is_owner(z - m if right else z + m)

    def full_targets(k, right):
        first = FULL_STRIDE * k + 1
        return range(first, min(first + FULL_STRIDE - 1, reach(n_sub, right)) + 1)

    def send_full(k, right):
        for m in reversed(full_targets(k, right)):
            hop = m - FULL_STRIDE * k
            pltpu.make_async_remote_copy(
                src_ref=held_slot(right, FULL_STRIDE * k), dst_ref=held_slot(right, m),
                send_sem=full_send, recv_sem=full_gather.at[lane(right, m)],
                device_id=in_ring(hop if right else -hop), device_id_type=MESH,
            ).start()

    def full_sent(k, right):
        for m in full_targets(k, right):
            wait_bytes(held_slot(right, 0), full_send)

    def full_arrived(right, m):
        @pl.when(origin(right, m))
        def _():
            wait_bytes(held_slot(right, m), full_gather.at[lane(right, m)])

    def by_origin(action):
        for k in range(2):
            for right in (True, False):
                if len(full_targets(k, right)):
                    pl.when(origin(right, FULL_STRIDE * k))(functools.partial(action, k, right))

    def to_core(ref):
        pltpu.make_async_remote_copy(
            src_ref=ref, dst_ref=ref, send_sem=core_sems.at[0], recv_sem=core_sems.at[1],
            device_id=partner, device_id_type=MESH,
        ).start()

    def pass_on(g):
        s, e = spans[g]
        ref = held.at[s * chunk:e * chunk]
        pltpu.make_async_remote_copy(
            src_ref=ref, dst_ref=ref, send_sem=hi_send, recv_sem=hi_gather.at[g],
            device_id=across, device_id_type=MESH,
        ).start()
        to_core(ref)

    near_r, near_l = (min(FULL_STRIDE, reach(n_sub, right)) for right in (True, False))
    spans = [(0, near_r + 1), (n_sub - near_l, n_sub), (near_r + 1, n_sub - near_l)]

    def pass_full(k, right):
        if k:
            wait_bytes(
                held_slot(right, FULL_STRIDE), full_gather.at[lane(right, FULL_STRIDE)]
            )
        send_full(k, right)

    by_origin(pass_full)
    for g, right in enumerate((True, False)):
        for m in range(1, min(FULL_STRIDE, reach(n_sub, right)) + 1):
            if m != FULL_STRIDE or m == reach(n_sub, right):
                full_arrived(right, m)
        if spans[g][0] < spans[g][1]:
            pass_on(g)
    for right in (True, False):
        for m in range(FULL_STRIDE + 1, reach(n_sub, right) + 1):
            full_arrived(right, m)
    if spans[2][0] < spans[2][1]:
        pass_on(2)
    for g, (s, e) in enumerate(spans):
        if s < e:
            ref = other.at[s * chunk:e * chunk]
            wait_bytes(ref, hi_gather.at[g])
            to_core(ref)
    wait_bytes(full.at[1 - core], core_sems.at[1])
    store = pltpu.make_async_copy(full, full_out, store_sem)
    store.start()
    store.wait()

    for w in range(2):
        wait_bytes(proj_recv.at[w], proj_sems.at[w, 0])
    wait_bytes(feat_all.at[0], feat_sems.at[0])
    wait_bytes(img_all.at[rows:half_img], img_send)
    wait_bytes(img_all.at[0:half_img], img_core.at[0])
    wait_bytes(txt_all.at[rows:n_txt], txt_send)
    wait_bytes(img_pair, img_pair_sems.at[0])
    wait_bytes(img_recv.at[0:(chips - 1) * rows], img_sum_sems.at[0])
    wait_bytes(txt_all.at[rows:n_txt], txt_sum_send)
    wait_bytes(back_all.at[0:(2 * n_tp - 1) * rows], back_sems.at[0])
    for i, (lo, up) in enumerate(parts):
        wait_bytes(half_send.at[lo * chunk:min(up * chunk, sent)], half_sems.at[i, 0])
    for d in range(1, n_sub):
        @pl.when(is_owner(z + d))
        def _():
            wait_bytes(grad_recv.at[0], grad_sems.at[0])
    by_origin(full_sent)
    wait_bytes(held, hi_send)
    wait_bytes(full.at[core], core_sems.at[0])


def lay_out(n_sub, half, tiles, full_hbm, outi_hbm, outt_hbm, full, ordered, both, load_sems, store_sems):
    z = lax.axis_index("sub")
    chunk = full.shape[2] // n_sub
    parts = [(w, h) for w in range(2) for h in range(2)]
    loads = [
        pltpu.make_async_copy(full_hbm.at[w, h], full.at[w, h], load_sems.at[w, h])
        for w, h in parts
    ]
    for load in loads:
        load.start()
    stores = []
    for (w, h), load in zip(parts, loads):
        load.wait()
        for d in range(n_sub):
            at = lax.rem(z - d + n_sub, n_sub) * chunk
            ordered[pl.ds(pl.multiple_of(at, chunk), chunk)] = (
                full[w, h, d * chunk:(d + 1) * chunk].astype(F32)
            )
        rows = slice(h * half, (h + 1) * half)
        for k in range(tiles):
            both[w, rows, k * 128:(k + 1) * 128] = ordered[k * half:(k + 1) * half]
        store = pltpu.make_async_copy(
            both.at[w, rows], (outi_hbm, outt_hbm)[w].at[rows], store_sems.at[w, h]
        )
        store.start()
        stores.append(store)
    for store in stores:
        store.wait()


def per_device(n_loop, n_sub, n_tp, img_feat, txt_feat, img_weight, txt_weight, scale, bias):
    depth, width = img_weight.shape
    batch = img_feat.shape[0]
    rows = batch // n_tp
    half_img, n_txt = n_loop // 2 * n_tp * rows, n_sub * rows
    n_img = 2 * half_img
    used = width // 128 * depth // 2
    chunk = up16(-(-used // n_sub))
    dma = pltpu.SemaphoreType.DMA
    smem = pl.BlockSpec(memory_space=pltpu.SMEM)
    hbm = pl.BlockSpec(memory_space=pltpu.HBM)
    full = pl.pallas_call(
        functools.partial(kernel, n_loop, n_sub, n_tp),
        out_shape=jax.ShapeDtypeStruct((2, 2, n_sub * chunk, 128), BF16),
        in_specs=[smem, smem] + [hbm] * 4,
        out_specs=hbm,
        scratch_shapes=[
            pltpu.VMEM((2, depth, batch), BF16),
            pltpu.VMEM((2, depth, width), BF16),
            pltpu.VMEM((2, batch, width), F32),
            pltpu.VMEM((2, n_tp - 1, rows, width), F32),
            pltpu.VMEM((n_img, width), BF16),
            pltpu.VMEM((n_txt, width), BF16),
            pltpu.VMEM((n_img, n_txt), BF16),
            pltpu.VMEM((n_img, width), BF16),
            pltpu.VMEM((n_txt, width), BF16),
            pltpu.VMEM((half_img, width), BF16),
            pltpu.VMEM((half_img, width), BF16),
            pltpu.VMEM((n_txt, width), BF16),
            pltpu.VMEM((rows, width), F32),
            pltpu.VMEM((rows, width), F32),
            pltpu.VMEM((2, rows, width), BF16),
            pltpu.VMEM((2 * batch, width), BF16),
            pltpu.VMEM((2, depth, batch), BF16),
            pltpu.VMEM((depth, width), F32),
            pltpu.VMEM((n_sub * chunk, 128), F32),
            pltpu.VMEM((up16(used), 128), BF16),
            pltpu.VMEM((up16(used), 128), BF16),
            pltpu.VMEM((n_sub * chunk, 128), BF16),
            pltpu.VMEM((n_sub - 1, chunk, 128), BF16),
            pltpu.VMEM((2, 2, n_sub * chunk, 128), BF16),
            dma((2, 2)),
            dma((2,)),
            dma((2, 2)),
            dma,
            dma((n_loop // 2 * n_tp,)),
            dma((2,)),
            dma,
            dma((n_sub,)),
            dma((2,)),
            dma((2,)),
            dma,
            dma((n_sub,)),
            dma((2,)),
            dma((2, 2)),
            dma((2,)),
            dma,
            dma((n_sub,)),
            dma,
            dma((3,)),
            dma((2,)),
            dma,
        ],
        compiler_params=pltpu.CompilerParams(
            collective_id=0, has_side_effects=True, vmem_limit_bytes=60 * 1024 * 1024
        ),
        cost_estimate=pl.CostEstimate(
            flops=6 * n_img * n_txt * width, bytes_accessed=4 * depth * width * 3, transcendentals=0
        ),
    )(scale, bias, img_feat.T, txt_feat.T, img_weight, txt_weight)
    out = jax.ShapeDtypeStruct((depth, width), F32)
    return pl.pallas_call(
        functools.partial(lay_out, n_sub, depth // 2, width // 128),
        out_shape=(out, out),
        in_specs=[hbm],
        out_specs=(hbm, hbm),
        scratch_shapes=[
            pltpu.VMEM((2, 2, n_sub * chunk, 128), BF16),
            pltpu.VMEM((n_sub * chunk, 128), F32),
            pltpu.VMEM((2, depth, width), F32),
            dma((2, 2)),
            dma((2, 2)),
        ],
        compiler_params=pltpu.CompilerParams(vmem_limit_bytes=60 * 1024 * 1024),
    )(full)


def solution(mesh):
    placed = (
        P(("loop", "sub"), "tp"),
        P(("loop", "sub"), "tp"),
        P("tp", None),
        P("tp", None),
        P(),
        P(),
    )
    sizes = (mesh.shape["loop"], mesh.shape["sub"], mesh.shape["tp"])
    return jax.shard_map(
        functools.partial(per_device, *sizes),
        mesh=mesh,
        in_specs=placed,
        out_specs=(P("tp", None), P("tp", None)),
        check_vma=False,
    )
```
